32 devices in a mesh: gy: 8 (over y, x, core), gx: 4 (over z).
Axes of the slice: x: 2, y: 2, z: 4, core: 2. Of those that a mesh axis runs over, the one named last changes fastest.
Arguments:
- features: bfloat16 [256, 256, 128], P('gy', 'gx'), may hold values from -6 to 6
- station_mask: int32 [256, 256], P('gy', 'gx'), may hold values 0 or 1
- station_gain: float32 [128], replicated, may hold values from -4 to 4
- fine_kernel: bfloat16 [3, 3, 128, 128], replicated, may hold values from -0.1875 to 0.1875
- down_mid: bfloat16 [128, 256], replicated, may hold values from -0.5 to 0.5
- mid_kernel: bfloat16 [3, 3, 256, 256], replicated, may hold values from -0.125 to 0.125
- down_coarse: bfloat16 [256, 512], replicated, may hold values from -0.375 to 0.375
- coarse_kernel: bfloat16 [3, 3, 512, 512], P(None, None, None, 'gx'), may hold values from -0.09375 to 0.09375
- up_coarse: bfloat16 [512, 256], replicated, may hold values from -0.25 to 0.25
- central_lifted_mixing: bfloat16 [256, 128], replicated, may hold values from -0.375 to 0.375
- cotangent: bfloat16 [256, 256, 128], P('gy', 'gx'), may hold values from -6 to 6
Outputs:
- predicted_rainfall: bfloat16 [256, 256, 128], P('gy', 'gx')
- hidden_maps_sensitivity: bfloat16 [256, 256, 128], P('gy', 'gx')
- sharpest_filter_derivative: float32 [3, 3, 128, 128], replicated
The draws below stay inside these ranges and needn't reach their ends.
All inputs are finite; a program needn't handle non-finite values. No bound on the sum of `station_mask` on one device may be relied on, other than what follows from the above.
Results may differ from the reference program's by a relative error of at most 0.0095.
Values may be sent and summed in bfloat16 or wider, within the bound.
A program may use at most 64 MiB of HBM per device.

```python
import jax
import jax.numpy as jnp
from jax import lax

C1 = 128
C2 = 256
C3 = 512
ROWS = 256
COLS = 256


def touch_ends(array, rng, smallest, largest):
    longest = array.shape.index(max(array.shape))
    spots = []
    for shift in (0, 1):
        where = [jax.random.randint(jax.random.fold_in(rng, axis), (), 0, length) for axis, length in enumerate(array.shape)]
        where[longest] = (where[longest] + shift) % array.shape[longest]
        spots.append(tuple(where))
    return array.at[spots[0]].set(smallest).at[spots[1]].set(largest)


def steps_of(key, dims, shards, smallest, top_value):
    factor_of, own = 1.0, jax.random.fold_in(key, 6)
    for position, parts in shards:
        heights = jnp.exp(jax.random.uniform(jax.random.fold_in(own, position), (parts,), jnp.float32, smallest / len(shards), top_value / len(shards)))
        factor_of = factor_of * jnp.repeat(heights, dims[position] // parts).reshape([-1 if axis == position else 1 for axis in range(len(dims))])
    return factor_of


def noise(key, extent, spread, limit, shards=(), dtype=jnp.bfloat16):
    values = jax.random.normal(key, extent, jnp.float32) * spread
    if len(shards) > 0:
        values = steps_of(key, extent, shards, -0.22, 0.18) * values
    return jnp.clip(values, min=-limit, max=limit).astype(dtype)


def setup_inputs(seed: int = 0) -> dict:
    streams_of = jax.random.split(jax.random.key(seed), 12)
    features = noise(streams_of[0], (ROWS, COLS, C1), 1.0, 6.0, ((0, 8), (1, 4)))
    station_mask = touch_ends((jax.random.randint(streams_of[1], (ROWS, COLS), 0, 4) < 1).astype(jnp.int32), jax.random.fold_in(streams_of[1], 1), 0, 1)
    station_gain = noise(streams_of[2], (C1,), 1.0, 4.0, (), jnp.float32)
    fine_kernel = noise(streams_of[3], (3, 3, C1, C1), (9 * C1) ** -0.5, 0.1875)
    down_mid = noise(streams_of[4], (C1, C2), C1 ** -0.5, 0.5)
    mid_kernel = noise(streams_of[5], (3, 3, C2, C2), (9 * C2) ** -0.5, 0.125)
    down_coarse = noise(streams_of[6], (C2, C3), C2 ** -0.5, 0.375)
    coarse_kernel = noise(streams_of[7], (3, 3, C3, C3), (9 * C3) ** -0.5, 0.09375, ((3, 4),))
    up_coarse = noise(streams_of[8], (C3, C2), C3 ** -0.5, 0.25)
    central_lifted_mixing = noise(streams_of[9], (C2, C1), C2 ** -0.5, 0.375)
    cotangent = noise(streams_of[10], (ROWS, COLS, C1), 1.0, 6.0, ((0, 8), (1, 4)))
    return dict(features=features, station_mask=station_mask, station_gain=station_gain, fine_kernel=fine_kernel, down_mid=down_mid, mid_kernel=mid_kernel, down_coarse=down_coarse, coarse_kernel=coarse_kernel, up_coarse=up_coarse, central_lifted_mixing=central_lifted_mixing, cotangent=cotangent)


def conv_valid(padded, kernel):
    rows = padded.shape[0] - 2
    cols = padded.shape[1] - 2
    total = jnp.zeros((rows * cols, kernel.shape[3]), jnp.float32)
    for row_off in range(3):
        for col_off in range(3):
            window = padded[row_off:row_off + rows, col_off:col_off + cols].reshape(rows * cols, -1)
            total = total + jnp.dot(window, kernel[row_off, col_off], preferred_element_type=jnp.float32)
    return total.reshape(rows, cols, kernel.shape[3])

def convt_valid(padded, kernel):
    rows = padded.shape[0] - 2
    cols = padded.shape[1] - 2
    total = jnp.zeros((rows * cols, kernel.shape[2]), jnp.float32)
    for row_off in range(3):
        for col_off in range(3):
            window = padded[2 - row_off:2 - row_off + rows, 2 - col_off:2 - col_off + cols].reshape(rows * cols, -1)
            total = total + lax.dot_general(window, kernel[row_off, col_off], (((1,), (1,)), ((), ())), preferred_element_type=jnp.float32)
    return total.reshape(rows, cols, kernel.shape[2])

def kernel_grad(padded, delta):
    rows = padded.shape[0] - 2
    cols = padded.shape[1] - 2
    flat_delta = delta.reshape(rows * cols, -1)
    blocks = []
    for row_off in range(3):
        line = []
        for col_off in range(3):
            window = padded[row_off:row_off + rows, col_off:col_off + cols].reshape(rows * cols, -1)
            line.append(lax.dot_general(window, flat_delta, (((0,), (0,)), ((), ())), preferred_element_type=jnp.float32))
        blocks.append(jnp.stack(line))
    return jnp.stack(blocks)

def pool_mean(field):
    rows, cols, chans = field.shape
    return field.astype(jnp.float32).reshape(rows // 2, 2, cols // 2, 2, chans).mean(axis=(1, 3)).astype(jnp.bfloat16)

def block_sum(field):
    rows, cols, chans = field.shape
    return field.astype(jnp.float32).reshape(rows // 2, 2, cols // 2, 2, chans).sum(axis=(1, 3))

def double_spatial_lattice(field):
    return jnp.repeat(jnp.repeat(field, 2, axis=0), 2, axis=1)

def pointwise_mixing_weights(field, matrix):
    rows, cols, chans = field.shape
    return jnp.dot(field.reshape(rows * cols, chans), matrix, preferred_element_type=jnp.float32).reshape(rows, cols, -1)

def project_back(field, matrix):
    rows, cols, chans = field.shape
    out = lax.dot_general(field.reshape(rows * cols, chans), matrix, (((1,), (1,)), ((), ())), preferred_element_type=jnp.float32)
    return out.reshape(rows, cols, -1)

def silu_slope(value):
    sig = jax.nn.sigmoid(value)
    return sig * (1.0 + value * (1.0 - sig))

def pad_one(field):
    return jnp.pad(field, ((1, 1), (1, 1), (0, 0)))

def reference(features, station_mask, station_gain, fine_kernel, down_mid, mid_kernel, down_coarse, coarse_kernel, up_coarse, central_lifted_mixing, cotangent):
    inputs = (features.astype(jnp.float32) + station_mask.astype(jnp.float32)[:, :, None] * station_gain[None, None, :]).astype(jnp.bfloat16)
    in_pad = pad_one(inputs)
    pre_fine = conv_valid(in_pad, fine_kernel)
    sharpest_level_response = jax.nn.silu(pre_fine).astype(jnp.bfloat16)
    mid_in = pointwise_mixing_weights(pool_mean(sharpest_level_response), down_mid).astype(jnp.bfloat16)
    pre_mid = conv_valid(pad_one(mid_in), mid_kernel)
    act_mid = jax.nn.silu(pre_mid).astype(jnp.bfloat16)
    coarse_in = pointwise_mixing_weights(pool_mean(act_mid), down_coarse).astype(jnp.bfloat16)
    pre_coarse = conv_valid(pad_one(coarse_in), coarse_kernel)
    act_coarse = jax.nn.silu(pre_coarse).astype(jnp.bfloat16)
    ascend_central_level = (double_spatial_lattice(pointwise_mixing_weights(act_coarse, up_coarse)) + act_mid.astype(jnp.float32)).astype(jnp.bfloat16)
    predicted_rainfall = (double_spatial_lattice(pointwise_mixing_weights(ascend_central_level, central_lifted_mixing)) + sharpest_level_response.astype(jnp.float32)).astype(jnp.bfloat16)
    back_mid = block_sum(cotangent).astype(jnp.bfloat16)
    grad_mid = project_back(back_mid, central_lifted_mixing)
    back_coarse = block_sum(grad_mid).astype(jnp.bfloat16)
    delta_coarse = (project_back(back_coarse, up_coarse) * silu_slope(pre_coarse)).astype(jnp.bfloat16)
    into_coarse = convt_valid(pad_one(delta_coarse), coarse_kernel).astype(jnp.bfloat16)
    delta_mid = ((grad_mid + double_spatial_lattice(project_back(into_coarse, down_coarse)) * 0.25) * silu_slope(pre_mid)).astype(jnp.bfloat16)
    into_mid = convt_valid(pad_one(delta_mid), mid_kernel).astype(jnp.bfloat16)
    delta_fine = ((cotangent.astype(jnp.float32) + double_spatial_lattice(project_back(into_mid, down_mid)) * 0.25) * silu_slope(pre_fine)).astype(jnp.bfloat16)
    scale = 1.0 / jnp.sqrt(jnp.float32(ROWS * COLS))
    sharpest_filter_derivative = kernel_grad(in_pad, delta_fine) * scale
    hidden_maps_sensitivity = convt_valid(pad_one(delta_fine), fine_kernel).astype(jnp.bfloat16)
    return (predicted_rainfall, hidden_maps_sensitivity, sharpest_filter_derivative)
```

```python
import functools

import jax
import jax.numpy as jnp
from jax import lax
from jax.experimental import pallas as pl
from jax.experimental.pallas import tpu as pltpu
from jax.sharding import PartitionSpec as P

MESH = pl.DeviceIdType.MESH
ANY = pl.BlockSpec(memory_space=pl.ANY)
VMEM = pl.BlockSpec(memory_space=pltpu.VMEM)

DIRS = ((-1, 0), (1, 0), (0, -1), (0, 1), (-1, -1), (-1, 1), (1, -1), (1, 1))
OPP = (1, 0, 3, 2, 7, 6, 5, 4)


def halo_kernel(ny, nx, rows_in, cols_in, corn_in, rows_out, cols_out, corn_out, send, recv):
    y, x = lax.axis_index("gy"), lax.axis_index("gx")

    def exists(d):
        dy, dx = DIRS[d]
        ok = True
        if dy < 0:
            ok = y > 0
        if dy > 0:
            ok = y < ny - 1
        if dx != 0:
            okx = x > 0 if dx < 0 else x < nx - 1
            ok = okx if dy == 0 else jnp.logical_and(ok, okx)
        return ok

    def part(d, rows, cols, corn):
        return rows.at[d] if d < 2 else cols.at[d - 2] if d < 4 else corn.at[d - 4]

    def copy(d):
        return pltpu.make_async_remote_copy(
            src_ref=part(d, rows_in, cols_in, corn_in),
            dst_ref=part(OPP[d], rows_out, cols_out, corn_out),
            send_sem=send.at[d],
            recv_sem=recv.at[OPP[d]],
            device_id=(y + DIRS[d][0], x + DIRS[d][1]),
            device_id_type=MESH,
        )

    def landing(d):
        return pltpu.make_async_remote_copy(
            src_ref=part(d, rows_in, cols_in, corn_in),
            dst_ref=part(d, rows_out, cols_out, corn_out),
            send_sem=send.at[d],
            recv_sem=recv.at[d],
            device_id=(y + DIRS[d][0], x + DIRS[d][1]),
            device_id_type=MESH,
        )

    barrier = pltpu.get_barrier_semaphore()
    for d in range(8):

        @pl.when(exists(d))
        def _(d=d):
            pl.semaphore_signal(
                barrier, inc=1, device_id=(y + DIRS[d][0], x + DIRS[d][1]), device_id_type=MESH
            )

    above_below = jnp.minimum(y, 1) + jnp.minimum(ny - 1 - y, 1)
    sideways = jnp.minimum(x, 1) + jnp.minimum(nx - 1 - x, 1)
    pl.semaphore_wait(barrier, (above_below + 1) * (sideways + 1) - 1)

    for d in range(8):

        @pl.when(exists(d))
        def _(d=d):
            copy(d).start()

    for d in range(8):

        @pl.when(exists(d))
        def _(d=d):
            copy(d).wait_send()
            landing(d).wait_recv()


def with_halo(x, call_id):
    h, w, c = x.shape
    ny, nx = lax.axis_size("gy"), lax.axis_size("gx")
    y, xx = lax.axis_index("gy"), lax.axis_index("gx")
    rows = jnp.stack([x[0], x[h - 1]])
    cols = jnp.stack([x[:, 0], x[:, w - 1]])
    corners = jnp.stack([x[0, 0], x[0, w - 1], x[h - 1, 0], x[h - 1, w - 1]])
    corners = jnp.broadcast_to(corners[:, None, :], (4, 16, c))
    rows, cols, corners = pl.pallas_call(
        functools.partial(halo_kernel, ny, nx),
        out_shape=[jax.ShapeDtypeStruct(a.shape, a.dtype) for a in (rows, cols, corners)],
        in_specs=[VMEM] * 3,
        out_specs=[VMEM] * 3,
        scratch_shapes=[pltpu.SemaphoreType.DMA((8,)), pltpu.SemaphoreType.DMA((8,))],
        compiler_params=pltpu.CompilerParams(collective_id=call_id, has_side_effects=True),
        name="halo",
    )(rows, cols, corners)
    zero = jnp.zeros((), x.dtype)
    has_y = jnp.stack([y > 0, y < ny - 1])
    has_x = jnp.stack([xx > 0, xx < nx - 1])
    rows = jnp.where(has_y[:, None, None], rows, zero)
    cols = jnp.where(has_x[:, None, None], cols, zero)
    has = (has_y[:, None] & has_x[None, :]).reshape(4)
    corners = jnp.where(has[:, None], corners[:, 0], zero)
    top = jnp.concatenate([corners[0][None], rows[0], corners[1][None]], axis=0)
    bottom = jnp.concatenate([corners[2][None], rows[1], corners[3][None]], axis=0)
    middle = jnp.concatenate([cols[0][:, None], x, cols[1][:, None]], axis=1)
    return jnp.concatenate([top[None], middle, bottom[None]], axis=0)


def strip_kernel(ny, nx, body_in, edge_in, body_out, edge_out, send, recv):
    y, x = lax.axis_index("gy"), lax.axis_index("gx")
    links = [(0, k) for k in range(1, nx)]
    links += [(dy, k) for dy in (-1, 1) for k in range(nx)]

    def when(dy, run):
        if dy == 0:
            run()
        else:
            pl.when(y > 0 if dy < 0 else y < ny - 1)(run)

    def copy(i, slot_of):
        dy, k = links[i]
        other = lax.rem(x + k, nx)
        if dy == 0:
            src, dst = body_in, body_out.at[slot_of(k)]
        else:
            src, dst = edge_in.at[0 if dy < 0 else 1], edge_out.at[1 if dy < 0 else 0, slot_of(k)]
        return pltpu.make_async_remote_copy(
            src_ref=src,
            dst_ref=dst,
            send_sem=send.at[i],
            recv_sem=recv.at[i],
            device_id=(y + dy, other),
            device_id_type=MESH,
        )

    def landing(i):
        dy, k = links[i]
        source = lax.rem(x - k + nx, nx)
        if dy == 0:
            src, dst = body_in, body_out.at[source]
        else:
            src, dst = edge_in.at[0 if dy < 0 else 1], edge_out.at[1 if dy < 0 else 0, source]
        return pltpu.make_async_remote_copy(
            src_ref=src,
            dst_ref=dst,
            send_sem=send.at[i],
            recv_sem=recv.at[i],
            device_id=(y - dy, source),
            device_id_type=MESH,
        )

    barrier = pltpu.get_barrier_semaphore()
    for dy, k in links:

        def greet(dy=dy, k=k):
            pl.semaphore_signal(
                barrier, inc=1, device_id=(y + dy, lax.rem(x + k, nx)), device_id_type=MESH
            )

        when(dy, greet)
    above_below = jnp.minimum(y, 1) + jnp.minimum(ny - 1 - y, 1)
    pl.semaphore_wait(barrier, nx - 1 + above_below * nx)
    for i in range(len(links)):
        when(links[i][0], lambda i=i: copy(i, lambda k: x).start())
    for i in range(len(links)):
        when(links[i][0], lambda i=i: copy(i, lambda k: x).wait_send())
        when(-links[i][0], lambda i=i: landing(i).wait_recv())


def gather_strip(block, reach, call_id):
    h, w, c = block.shape
    ny, nx = lax.axis_size("gy"), lax.axis_size("gx")
    y, x = lax.axis_index("gy"), lax.axis_index("gx")
    body = block.reshape(h * w, c)
    edges = jnp.stack([block[:reach], block[h - reach :]]).reshape(2, reach * w, c)
    count = nx - 1 + 2 * nx
    got, rims = pl.pallas_call(
        functools.partial(strip_kernel, ny, nx),
        out_shape=[
            jax.ShapeDtypeStruct((nx, h * w, c), block.dtype),
            jax.ShapeDtypeStruct((2, nx, reach * w, c), block.dtype),
        ],
        in_specs=[VMEM] * 2,
        out_specs=[VMEM] * 2,
        scratch_shapes=[pltpu.SemaphoreType.DMA((count,)), pltpu.SemaphoreType.DMA((count,))],
        compiler_params=pltpu.CompilerParams(collective_id=call_id, has_side_effects=True),
        name="strip",
    )(body, edges)
    zero = jnp.zeros((), block.dtype)
    mine = (jnp.arange(nx) == x)[:, None, None]
    got = jnp.where(mine, body[None], got).reshape(nx, h, w, c)
    has = jnp.stack([y > 0, y < ny - 1])[:, None, None, None]
    rims = jnp.where(has, rims, zero).reshape(2, nx, reach, w, c)
    full = jnp.concatenate([rims[0], got, rims[1]], axis=1)
    return full.transpose(1, 0, 2, 3).reshape(h + 2 * reach, nx * w, c)


def swap_kernel(nx, blocks, out, send, recv):
    y, x = lax.axis_index("gy"), lax.axis_index("gx")

    def copy(k, src_slot, dst_slot, device):
        return pltpu.make_async_remote_copy(
            src_ref=blocks.at[src_slot],
            dst_ref=out.at[dst_slot],
            send_sem=send.at[k],
            recv_sem=recv.at[k],
            device_id=(y, device),
            device_id_type=MESH,
        )

    barrier = pltpu.get_barrier_semaphore()
    for k in range(1, nx):
        pl.semaphore_signal(
            barrier, inc=1, device_id=(y, lax.rem(x + k, nx)), device_id_type=MESH
        )
    pl.semaphore_wait(barrier, nx - 1)
    for k in range(1, nx):
        to = lax.rem(x + k, nx)
        copy(k, to, x, to).start()
    for k in range(1, nx):
        to = lax.rem(x + k, nx)
        source = lax.rem(x - k + nx, nx)
        copy(k, to, x, to).wait_send()
        copy(k, to, source, source).wait_recv()


def swap_blocks(blocks, call_id):
    nx = lax.axis_size("gx")
    got = pl.pallas_call(
        functools.partial(swap_kernel, nx),
        out_shape=jax.ShapeDtypeStruct(blocks.shape, blocks.dtype),
        in_specs=[VMEM],
        out_specs=VMEM,
        scratch_shapes=[pltpu.SemaphoreType.DMA((nx,)), pltpu.SemaphoreType.DMA((nx,))],
        compiler_params=pltpu.CompilerParams(collective_id=call_id, has_side_effects=True),
        name="swap",
    )(blocks)
    mine = (jnp.arange(nx) == lax.axis_index("gx"))[:, None, None]
    return jnp.where(mine, blocks, got)


def sum_kernel(ny, nx, src, out, got_y, got_x, s1, r1, s2, r2, s3, r3):
    y, x = lax.axis_index("gy"), lax.axis_index("gx")
    f32 = jnp.float32

    def copy(a, b, s, r, device):
        return pltpu.make_async_remote_copy(
            src_ref=a, dst_ref=b, send_sem=s, recv_sem=r, device_id=device, device_id_type=MESH
        )

    def over_y(k):
        return (lax.rem(y + k, ny), x)

    def over_x(k):
        return (y, lax.rem(x + k, nx))

    barrier = pltpu.get_barrier_semaphore()
    for k in range(1, ny):
        pl.semaphore_signal(barrier, inc=1, device_id=over_y(k), device_id_type=MESH)
    for k in range(1, nx):
        pl.semaphore_signal(barrier, inc=1, device_id=over_x(k), device_id_type=MESH)
    pl.semaphore_wait(barrier, ny + nx - 2)

    for k in range(1, ny):
        to = over_y(k)
        copy(src.at[to[0]], got_y.at[k], s1.at[k], r1.at[k], to).start()
    total = src[y].astype(f32)
    for k in range(1, ny):
        to = over_y(k)
        copy(src.at[to[0]], got_y.at[k], s1.at[k], r1.at[k], to).wait()
        total = total + got_y[k].astype(f32)
    got_x[x] = total.astype(got_x.dtype)

    for k in range(1, nx):
        copy(got_x.at[x], got_x.at[x], s2.at[k], r2.at[k], over_x(k)).start()
    for k in range(1, nx):
        source = lax.rem(x - k + nx, nx)
        copy(got_x.at[x], got_x.at[x], s2.at[k], r2.at[k], over_x(k)).wait_send()
        copy(got_x.at[x], got_x.at[source], s2.at[k], r2.at[k], over_x(k)).wait_recv()
    total = got_x[0].astype(f32)
    for p in range(1, nx):
        total = total + got_x[p].astype(f32)
    out[y] = total.astype(out.dtype)

    for k in range(1, ny):
        copy(out.at[y], out.at[y], s3.at[k], r3.at[k], over_y(k)).start()
    for k in range(1, ny):
        source = lax.rem(y - k + ny, ny)
        copy(out.at[y], out.at[y], s3.at[k], r3.at[k], over_y(k)).wait_send()
        copy(out.at[y], out.at[source], s3.at[k], r3.at[k], over_y(k)).wait_recv()


def sum_all(term, call_id):
    ny, nx = lax.axis_size("gy"), lax.axis_size("gx")
    lanes = term.shape[-1]
    flat = term.reshape(-1, lanes)
    part = -(-flat.shape[0] // ny)
    part = -(-part // 16) * 16
    padded = jnp.pad(flat.astype(jnp.bfloat16), ((0, part * ny - flat.shape[0]), (0, 0)))
    blocks = padded.reshape(ny, part, lanes)
    dma = pltpu.SemaphoreType.DMA
    total = pl.pallas_call(
        functools.partial(sum_kernel, ny, nx),
        out_shape=jax.ShapeDtypeStruct(blocks.shape, blocks.dtype),
        in_specs=[VMEM],
        out_specs=VMEM,
        scratch_shapes=[
            pltpu.VMEM((ny, part, lanes), jnp.bfloat16),
            pltpu.VMEM((nx, part, lanes), jnp.bfloat16),
            dma((ny,)),
            dma((ny,)),
            dma((nx,)),
            dma((nx,)),
            dma((ny,)),
            dma((ny,)),
        ],
        compiler_params=pltpu.CompilerParams(collective_id=call_id, has_side_effects=True),
        name="sum_all",
    )(blocks)
    return total.reshape(ny * part, lanes)[: flat.shape[0]].reshape(term.shape)


def conv_valid(padded, kernel):
    rows = padded.shape[0] - 2
    cols = padded.shape[1] - 2
    total = jnp.zeros((rows * cols, kernel.shape[3]), jnp.float32)
    for row_off in range(3):
        for col_off in range(3):
            window = padded[row_off : row_off + rows, col_off : col_off + cols].reshape(
                rows * cols, -1
            )
            total = total + jnp.dot(
                window, kernel[row_off, col_off], preferred_element_type=jnp.float32
            )
    return total.reshape(rows, cols, kernel.shape[3])


def convt_valid(padded, kernel):
    rows = padded.shape[0] - 2
    cols = padded.shape[1] - 2
    total = jnp.zeros((rows * cols, kernel.shape[2]), jnp.float32)
    for row_off in range(3):
        for col_off in range(3):
            window = padded[
                2 - row_off : 2 - row_off + rows, 2 - col_off : 2 - col_off + cols
            ].reshape(rows * cols, -1)
            total = total + lax.dot_general(
                window,
                kernel[row_off, col_off],
                (((1,), (1,)), ((), ())),
                preferred_element_type=jnp.float32,
            )
    return total.reshape(rows, cols, kernel.shape[2])


def kernel_grad(padded, delta):
    rows = padded.shape[0] - 2
    cols = padded.shape[1] - 2
    flat_delta = delta.reshape(rows * cols, -1)
    blocks = []
    for row_off in range(3):
        line = []
        for col_off in range(3):
            window = padded[row_off : row_off + rows, col_off : col_off + cols].reshape(
                rows * cols, -1
            )
            line.append(
                lax.dot_general(
                    window, flat_delta, (((0,), (0,)), ((), ())), preferred_element_type=jnp.float32
                )
            )
        blocks.append(jnp.stack(line))
    return jnp.stack(blocks)


def pool_mean(field):
    rows, cols, chans = field.shape
    return (
        field.astype(jnp.float32)
        .reshape(rows // 2, 2, cols // 2, 2, chans)
        .mean(axis=(1, 3))
        .astype(jnp.bfloat16)
    )


def block_sum(field):
    rows, cols, chans = field.shape
    return field.astype(jnp.float32).reshape(rows // 2, 2, cols // 2, 2, chans).sum(axis=(1, 3))


def double_spatial_lattice(field):
    return jnp.repeat(jnp.repeat(field, 2, axis=0), 2, axis=1)


def pointwise_mixing_weights(field, matrix):
    rows, cols, chans = field.shape
    return jnp.dot(
        field.reshape(rows * cols, chans), matrix, preferred_element_type=jnp.float32
    ).reshape(rows, cols, -1)


def project_back(field, matrix):
    rows, cols, chans = field.shape
    out = lax.dot_general(
        field.reshape(rows * cols, chans),
        matrix,
        (((1,), (1,)), ((), ())),
        preferred_element_type=jnp.float32,
    )
    return out.reshape(rows, cols, -1)


def silu_slope(value):
    sig = jax.nn.sigmoid(value)
    return sig * (1.0 + value * (1.0 - sig))


def backward_start(cotangent, central_lifted_mixing):
    back_mid = block_sum(cotangent).astype(jnp.bfloat16)
    grad_mid = project_back(back_mid, central_lifted_mixing)
    return grad_mid, block_sum(grad_mid).astype(jnp.bfloat16)


def shards(
    features,
    station_mask,
    station_gain,
    fine_kernel,
    down_mid,
    mid_kernel,
    down_coarse,
    coarse_kernel,
    up_coarse,
    central_lifted_mixing,
    cotangent,
):
    inputs = (
        features.astype(jnp.float32)
        + station_mask.astype(jnp.float32)[:, :, None] * station_gain[None, None, :]
    ).astype(jnp.bfloat16)
    in_pad = with_halo(inputs, 0)
    pre_fine = conv_valid(in_pad, fine_kernel)
    sharpest_level_response = jax.nn.silu(pre_fine).astype(jnp.bfloat16)
    mid_in = pointwise_mixing_weights(pool_mean(sharpest_level_response), down_mid).astype(
        jnp.bfloat16
    )
    pre_mid = conv_valid(with_halo(mid_in, 1), mid_kernel)
    act_mid = jax.nn.silu(pre_mid).astype(jnp.bfloat16)
    grad_mid, back_coarse = backward_start(cotangent, central_lifted_mixing)
    x = lax.axis_index("gx")
    nx = lax.axis_size("gx")
    own_chans = coarse_kernel.shape[3]
    own_up = lax.dynamic_slice_in_dim(up_coarse, x * own_chans, own_chans, axis=0)
    pooled_mid = pool_mean(act_mid)
    rows, cols, chans = pooled_mid.shape
    strip = gather_strip(jnp.concatenate([pooled_mid, back_coarse], axis=2), 2, 2)
    coarse_in = pointwise_mixing_weights(strip[:, :, :chans], down_coarse).astype(jnp.bfloat16)
    pre_coarse = conv_valid(jnp.pad(coarse_in, ((0, 0), (1, 1), (0, 0))), coarse_kernel)
    act_own = jax.nn.silu(pre_coarse[1 : 1 + rows]).astype(jnp.bfloat16)
    delta_coarse = (
        project_back(strip[1 : 3 + rows, :, chans:], own_up) * silu_slope(pre_coarse)
    ).astype(jnp.bfloat16)
    into_own = convt_valid(
        jnp.pad(delta_coarse, ((0, 0), (1, 1), (0, 0))), coarse_kernel
    ).astype(jnp.bfloat16)
    down_own = project_back(into_own, down_coarse).astype(jnp.bfloat16)
    blocks = jnp.concatenate([act_own, down_own], axis=2)
    blocks = blocks.reshape(rows, nx, cols, -1).transpose(1, 0, 2, 3).reshape(nx, rows * cols, -1)
    blocks = swap_blocks(blocks, 3)
    act_coarse = blocks[:, :, :own_chans].transpose(1, 0, 2).reshape(rows, cols, nx * own_chans)
    down_back = blocks[:, :, own_chans:].astype(jnp.float32).sum(axis=0).reshape(rows, cols, -1)
    ascend_central_level = (
        double_spatial_lattice(pointwise_mixing_weights(act_coarse, up_coarse))
        + act_mid.astype(jnp.float32)
    ).astype(jnp.bfloat16)
    predicted_rainfall = (
        double_spatial_lattice(
            pointwise_mixing_weights(ascend_central_level, central_lifted_mixing)
        )
        + sharpest_level_response.astype(jnp.float32)
    ).astype(jnp.bfloat16)
    delta_mid = (
        (grad_mid + double_spatial_lattice(down_back) * 0.25)
        * silu_slope(pre_mid)
    ).astype(jnp.bfloat16)
    into_mid = convt_valid(with_halo(delta_mid, 4), mid_kernel).astype(jnp.bfloat16)
    delta_fine = (
        (
            cotangent.astype(jnp.float32)
            + double_spatial_lattice(project_back(into_mid, down_mid)) * 0.25
        )
        * silu_slope(pre_fine)
    ).astype(jnp.bfloat16)
    local_grad = kernel_grad(in_pad, delta_fine)
    cells_all = features.shape[0] * lax.axis_size("gy") * features.shape[1] * lax.axis_size("gx")
    scale = 1.0 / jnp.sqrt(jnp.float32(cells_all))
    sharpest_filter_derivative = sum_all(local_grad, 6).astype(jnp.float32) * scale
    hidden_maps_sensitivity = convt_valid(with_halo(delta_fine, 5), fine_kernel).astype(jnp.bfloat16)
    return (predicted_rainfall, hidden_maps_sensitivity, sharpest_filter_derivative)


def solution(mesh):
    return jax.shard_map(
        shards,
        mesh=mesh,
        in_specs=(
            P("gy", "gx", None),
            P("gy", "gx"),
            P(),
            P(),
            P(),
            P(),
            P(),
            P(None, None, None, "gx"),
            P(),
            P(),
            P("gy", "gx", None),
        ),
        out_specs=(P("gy", "gx", None), P("gy", "gx", None), P()),
        check_vma=False,
    )
```

```python
import functools

import jax
import jax.numpy as jnp
from jax import lax
from jax.experimental import pallas as pl
from jax.experimental.pallas import tpu as pltpu
from jax.sharding import PartitionSpec as P

MESH = pl.DeviceIdType.MESH
VMEM = pl.BlockSpec(memory_space=pltpu.VMEM)

DIRS = ((-1, 0), (1, 0), (0, -1), (0, 1), (-1, -1), (-1, 1), (1, -1), (1, 1))
OPP = (1, 0, 3, 2, 7, 6, 5, 4)


class Halo:
    def __init__(self, ny, nx, x_ref, cols_in, rows, cols, corners, send, recv):
        self.y, self.x = lax.axis_index("gy"), lax.axis_index("gx")
        self.ny, self.nx = ny, nx
        self.x_ref, self.cols_in = x_ref, cols_in
        self.out = (rows, cols, corners)
        self.send, self.recv = send, recv

    def exists(self, d):
        dy, dx = DIRS[d]
        y, x = self.y, self.x
        oky = None if dy == 0 else y > 0 if dy < 0 else y < self.ny - 1
        okx = None if dx == 0 else x > 0 if dx < 0 else x < self.nx - 1
        if oky is None:
            return okx
        return oky if okx is None else jnp.logical_and(oky, okx)

    def device(self, d):
        return (self.y + DIRS[d][0], self.x + DIRS[d][1])

    def source(self, d):
        h, w, _ = self.x_ref.shape
        dy, dx = DIRS[d]
        if d in (2, 3):
            return self.cols_in.at[d - 2]
        row = 0 if dy < 0 else h - 1
        if d < 2:
            return self.x_ref.at[row]
        return self.x_ref.at[row, pl.ds(0 if dx < 0 else w - 16, 16)]

    def slot(self, d):
        rows, cols, corners = self.out
        return rows.at[d] if d < 2 else cols.at[d - 2] if d < 4 else corners.at[d - 4]

    def copy(self, d, slot):
        return pltpu.make_async_remote_copy(
            src_ref=self.source(d),
            dst_ref=self.slot(slot),
            send_sem=self.send.at[d],
            recv_sem=self.recv.at[slot],
            device_id=self.device(d),
            device_id_type=MESH,
        )

    def greet(self, barrier):
        for d in range(8):

            @pl.when(self.exists(d))
            def _(d=d):
                pl.semaphore_signal(
                    barrier, inc=1, device_id=self.device(d), device_id_type=MESH
                )

        above_below = jnp.minimum(self.y, 1) + jnp.minimum(self.ny - 1 - self.y, 1)
        sideways = jnp.minimum(self.x, 1) + jnp.minimum(self.nx - 1 - self.x, 1)
        return (above_below + 1) * (sideways + 1) - 1

    def start(self):
        for d in range(8):

            @pl.when(self.exists(d))
            def _(d=d):
                self.copy(d, OPP[d]).start()

            @pl.when(jnp.logical_not(self.exists(d)))
            def _(d=d):
                slot = self.slot(d)
                slot[...] = jnp.zeros(slot.shape, slot.dtype)

    def wait(self):
        for d in range(8):

            @pl.when(self.exists(d))
            def _(d=d):
                self.copy(d, OPP[d]).wait_send()
                self.copy(d, d).wait_recv()

    def assemble(self, out):
        h, w, _ = self.x_ref.shape
        rows, cols, corners = self.out

        def edge(i):
            left, right = corners[2 * i].astype(jnp.float32), corners[2 * i + 1].astype(jnp.float32)
            line = [left[15:16], rows[i].astype(jnp.float32), right[0:1]]
            return jnp.concatenate(line, axis=0).astype(out.dtype)

        out[0] = edge(0)
        out[h + 1] = edge(1)
        left = cols[0].astype(jnp.float32)[:, None, :]
        right = cols[1].astype(jnp.float32)[:, None, :]
        middle = self.x_ref[...].astype(jnp.float32)
        out[1 : h + 1] = jnp.concatenate([left, middle, right], axis=1).astype(out.dtype)


class Strip:
    def __init__(self, ny, nx, block, out, send, recv):
        self.y, self.x = lax.axis_index("gy"), lax.axis_index("gx")
        self.ny, self.nx = ny, nx
        self.block, self.out, self.send, self.recv = block, out, send, recv
        self.reach = (out.shape[0] - block.shape[0]) // 2
        self.links = strip_links(nx)

    def when(self, dy, run):
        if dy == 0:
            run()
        else:
            pl.when(self.y > 0 if dy < 0 else self.y < self.ny - 1)(run)

    def copy(self, i, slot, device):
        dy, _ = self.links[i]
        h, w, _ = self.block.shape
        r = self.reach
        cols = pl.ds(pl.multiple_of(slot * w, w), w)
        if dy == 0:
            src, dst = self.block, self.out.at[pl.ds(r, h), cols]
        elif dy < 0:
            src, dst = self.block.at[pl.ds(0, r)], self.out.at[pl.ds(r + h, r), cols]
        else:
            src, dst = self.block.at[pl.ds(h - r, r)], self.out.at[pl.ds(0, r), cols]
        return pltpu.make_async_remote_copy(
            src_ref=src,
            dst_ref=dst,
            send_sem=self.send.at[i],
            recv_sem=self.recv.at[i],
            device_id=device,
            device_id_type=MESH,
        )

    def target(self, i):
        dy, k = self.links[i]
        return (self.y + dy, lax.rem(self.x + k, self.nx))

    def origin(self, i):
        dy, k = self.links[i]
        return (self.y - dy, lax.rem(self.x - k + self.nx, self.nx))

    def greet(self, barrier):
        for i, (dy, _) in enumerate(self.links):

            def signal(i=i):
                pl.semaphore_signal(
                    barrier, inc=1, device_id=self.target(i), device_id_type=MESH
                )

            self.when(dy, signal)
        above_below = jnp.minimum(self.y, 1) + jnp.minimum(self.ny - 1 - self.y, 1)
        return self.nx - 1 + above_below * self.nx

    def start(self):
        for i, (dy, _) in enumerate(self.links):
            self.when(dy, lambda i=i: self.copy(i, self.x, self.target(i)).start())
        h, w, c = self.block.shape
        r = self.reach
        cols = pl.ds(pl.multiple_of(self.x * w, w), w)
        self.out[r : r + h, cols, :] = self.block[...]
        rim = jnp.zeros((r, self.nx * w, c), self.out.dtype)

        @pl.when(self.y == 0)
        def _():
            self.out[:r] = rim

        @pl.when(self.y == self.ny - 1)
        def _():
            self.out[r + h :] = rim

    def wait(self):
        for i, (dy, _) in enumerate(self.links):
            self.when(dy, lambda i=i: self.copy(i, self.x, self.target(i)).wait_send())
            self.when(
                -dy, lambda i=i: self.copy(i, self.origin(i)[1], self.origin(i)).wait_recv()
            )


def strip_links(nx):
    return [(0, k) for k in range(1, nx)] + [(dy, k) for dy in (-1, 1) for k in range(nx)]


def strip_sems(nx):
    return [pltpu.SemaphoreType.DMA((len(strip_links(nx)),))] * 2


def strip_shape(block, reach, nx):
    h, w, c = block.shape
    return jax.ShapeDtypeStruct((h + 2 * reach, w * nx, c), block.dtype)


def halo_scratch(x):
    h, w, c = x.shape
    shapes = [(2, w, c), (2, h, c), (4, 16, c)]
    return [pltpu.VMEM(a, x.dtype) for a in shapes] + [pltpu.SemaphoreType.DMA((8,))] * 2


def halo_shape(x):
    h, w, c = x.shape
    return jax.ShapeDtypeStruct((h + 2, w + 2, c), x.dtype)


def halo_cols(x):
    w = x.shape[1]
    return jnp.concatenate([x[:, :1], x[:, w - 1 :]], axis=1).transpose(1, 0, 2)


def halo_kernel(ny, nx, field, cols_in, out, *scratch):
    halo = Halo(ny, nx, field, cols_in, *scratch)
    barrier = pltpu.get_barrier_semaphore()
    pl.semaphore_wait(barrier, halo.greet(barrier))
    halo.start()
    halo.wait()
    halo.assemble(out)


def with_halo(x, call_id):
    ny, nx = lax.axis_size("gy"), lax.axis_size("gx")
    return pl.pallas_call(
        functools.partial(halo_kernel, ny, nx),
        out_shape=halo_shape(x),
        in_specs=[VMEM] * 2,
        out_specs=VMEM,
        scratch_shapes=halo_scratch(x),
        compiler_params=pltpu.CompilerParams(collective_id=call_id, has_side_effects=True),
        name="halo",
    )(x, halo_cols(x))


def first_kernel(ny, nx, field, cols_in, block, out, strip_out, *scratch):
    halo = Halo(ny, nx, field, cols_in, *scratch[:5])
    strip = Strip(ny, nx, block, strip_out, *scratch[5:])
    barrier = pltpu.get_barrier_semaphore()
    pl.semaphore_wait(barrier, halo.greet(barrier) + strip.greet(barrier))
    halo.start()
    strip.start()
    halo.wait()
    halo.assemble(out)
    strip.wait()


def with_halo_and_strip(x, block, reach, call_id):
    ny, nx = lax.axis_size("gy"), lax.axis_size("gx")
    return pl.pallas_call(
        functools.partial(first_kernel, ny, nx),
        out_shape=[halo_shape(x), strip_shape(block, reach, nx)],
        in_specs=[VMEM] * 3,
        out_specs=[VMEM] * 2,
        scratch_shapes=halo_scratch(x) + strip_sems(nx),
        compiler_params=pltpu.CompilerParams(collective_id=call_id, has_side_effects=True),
        name="halo_strip",
    )(x, halo_cols(x), block)


def strip_kernel(ny, nx, block, out, send, recv):
    strip = Strip(ny, nx, block, out, send, recv)
    barrier = pltpu.get_barrier_semaphore()
    pl.semaphore_wait(barrier, strip.greet(barrier))
    strip.start()
    strip.wait()


def gather_strip(block, reach, call_id):
    ny, nx = lax.axis_size("gy"), lax.axis_size("gx")
    return pl.pallas_call(
        functools.partial(strip_kernel, ny, nx),
        out_shape=strip_shape(block, reach, nx),
        in_specs=[VMEM],
        out_specs=VMEM,
        scratch_shapes=strip_sems(nx),
        compiler_params=pltpu.CompilerParams(collective_id=call_id, has_side_effects=True),
        name="strip",
    )(block)


def swap_kernel(nx, blocks, out, send, recv):
    y, x = lax.axis_index("gy"), lax.axis_index("gx")

    def copy(k, src_slot, dst_slot, device):
        return pltpu.make_async_remote_copy(
            src_ref=blocks.at[src_slot],
            dst_ref=out.at[dst_slot],
            send_sem=send.at[k],
            recv_sem=recv.at[k],
            device_id=(y, device),
            device_id_type=MESH,
        )

    barrier = pltpu.get_barrier_semaphore()
    for k in range(1, nx):
        pl.semaphore_signal(
            barrier, inc=1, device_id=(y, lax.rem(x + k, nx)), device_id_type=MESH
        )
    pl.semaphore_wait(barrier, nx - 1)
    for k in range(1, nx):
        to = lax.rem(x + k, nx)
        copy(k, to, x, to).start()
    out[x] = blocks[x]
    for k in range(1, nx):
        to = lax.rem(x + k, nx)
        source = lax.rem(x - k + nx, nx)
        copy(k, to, x, to).wait_send()
        copy(k, to, source, source).wait_recv()


def swap_blocks(blocks, call_id):
    nx = lax.axis_size("gx")
    return pl.pallas_call(
        functools.partial(swap_kernel, nx),
        out_shape=jax.ShapeDtypeStruct(blocks.shape, blocks.dtype),
        in_specs=[VMEM],
        out_specs=VMEM,
        scratch_shapes=[pltpu.SemaphoreType.DMA((nx,)), pltpu.SemaphoreType.DMA((nx,))],
        compiler_params=pltpu.CompilerParams(collective_id=call_id, has_side_effects=True),
        name="swap",
    )(blocks)


def sum_kernel(ny, nx, src, field, cols_in, out, field_out, got_y, got_x, *scratch):
    s1, r1, s2, r2, s3, r3 = scratch[:6]
    y, x = lax.axis_index("gy"), lax.axis_index("gx")
    f32 = jnp.float32
    halo = Halo(ny, nx, field, cols_in, *scratch[6:])

    def copy(a, b, s, r, device):
        return pltpu.make_async_remote_copy(
            src_ref=a, dst_ref=b, send_sem=s, recv_sem=r, device_id=device, device_id_type=MESH
        )

    def over_y(k):
        return (lax.rem(y + k, ny), x)

    def over_x(k):
        return (y, lax.rem(x + k, nx))

    barrier = pltpu.get_barrier_semaphore()
    for k in range(1, ny):
        pl.semaphore_signal(barrier, inc=1, device_id=over_y(k), device_id_type=MESH)
    for k in range(1, nx):
        pl.semaphore_signal(barrier, inc=1, device_id=over_x(k), device_id_type=MESH)
    pl.semaphore_wait(barrier, halo.greet(barrier) + ny + nx - 2)
    halo.start()

    for k in range(1, ny):
        to = over_y(k)
        copy(src.at[to[0]], got_y.at[k], s1.at[k], r1.at[k], to).start()
    total = src[y].astype(f32)
    for k in range(1, ny):
        to = over_y(k)
        copy(src.at[to[0]], got_y.at[k], s1.at[k], r1.at[k], to).wait()
        total = total + got_y[k].astype(f32)
    got_x[x] = total.astype(got_x.dtype)

    for k in range(1, nx):
        copy(got_x.at[x], got_x.at[x], s2.at[k], r2.at[k], over_x(k)).start()
    halo.wait()
    halo.assemble(field_out)
    for k in range(1, nx):
        source = lax.rem(x - k + nx, nx)
        copy(got_x.at[x], got_x.at[x], s2.at[k], r2.at[k], over_x(k)).wait_send()
        copy(got_x.at[x], got_x.at[source], s2.at[k], r2.at[k], over_x(k)).wait_recv()
    total = got_x[0].astype(f32)
    for p in range(1, nx):
        total = total + got_x[p].astype(f32)
    out[y] = total.astype(out.dtype)

    for k in range(1, ny):
        copy(out.at[y], out.at[y], s3.at[k], r3.at[k], over_y(k)).start()
    for k in range(1, ny):
        source = lax.rem(y - k + ny, ny)
        copy(out.at[y], out.at[y], s3.at[k], r3.at[k], over_y(k)).wait_send()
        copy(out.at[y], out.at[source], s3.at[k], r3.at[k], over_y(k)).wait_recv()


def sum_all_with_halo(term, field, call_id):
    ny, nx = lax.axis_size("gy"), lax.axis_size("gx")
    lanes = term.shape[-1]
    flat = term.reshape(-1, lanes)
    part = -(-flat.shape[0] // ny)
    part = -(-part // 16) * 16
    padded = jnp.pad(flat.astype(jnp.bfloat16), ((0, part * ny - flat.shape[0]), (0, 0)))
    blocks = padded.reshape(ny, part, lanes)
    dma = pltpu.SemaphoreType.DMA
    total, padded_field = pl.pallas_call(
        functools.partial(sum_kernel, ny, nx),
        out_shape=[jax.ShapeDtypeStruct(blocks.shape, blocks.dtype), halo_shape(field)],
        in_specs=[VMEM] * 3,
        out_specs=[VMEM] * 2,
        scratch_shapes=[
            pltpu.VMEM((ny, part, lanes), jnp.bfloat16),
            pltpu.VMEM((nx, part, lanes), jnp.bfloat16),
            dma((ny,)),
            dma((ny,)),
            dma((nx,)),
            dma((nx,)),
            dma((ny,)),
            dma((ny,)),
        ]
        + halo_scratch(field),
        compiler_params=pltpu.CompilerParams(collective_id=call_id, has_side_effects=True),
        name="sum_all",
    )(blocks, field, halo_cols(field))
    total = total.reshape(ny * part, lanes)[: flat.shape[0]].reshape(term.shape)
    return total, padded_field


def conv_valid(padded, kernel, side=0):
    return lax.conv_general_dilated(
        padded[None],
        kernel,
        window_strides=(1, 1),
        padding=((0, 0), (side, side)),
        dimension_numbers=("NHWC", "HWIO", "NHWC"),
        preferred_element_type=jnp.float32,
    )[0]


def convt_valid(padded, kernel, side=0):
    return lax.conv_general_dilated(
        padded[None],
        kernel[::-1, ::-1],
        window_strides=(1, 1),
        padding=((0, 0), (side, side)),
        dimension_numbers=("NHWC", "HWOI", "NHWC"),
        preferred_element_type=jnp.float32,
    )[0]


def kernel_grad(padded, delta):
    rows = padded.shape[0] - 2
    cols = padded.shape[1] - 2
    flat_delta = delta.reshape(rows * cols, -1)
    blocks = []
    for row_off in range(3):
        line = []
        for col_off in range(3):
            window = padded[row_off : row_off + rows, col_off : col_off + cols].reshape(
                rows * cols, -1
            )
            line.append(
                lax.dot_general(
                    window, flat_delta, (((0,), (0,)), ((), ())), preferred_element_type=jnp.float32
                )
            )
        blocks.append(jnp.stack(line))
    return jnp.stack(blocks)


def pool_mean(field):
    rows, cols, chans = field.shape
    return (
        field.astype(jnp.float32)
        .reshape(rows // 2, 2, cols // 2, 2, chans)
        .mean(axis=(1, 3))
        .astype(jnp.bfloat16)
    )


def block_sum(field):
    rows, cols, chans = field.shape
    return field.astype(jnp.float32).reshape(rows // 2, 2, cols // 2, 2, chans).sum(axis=(1, 3))


def double_spatial_lattice(field):
    return jnp.repeat(jnp.repeat(field, 2, axis=0), 2, axis=1)


def up_mix(field, matrix):
    taps = jnp.broadcast_to(matrix, (2, 2) + matrix.shape)
    return lax.conv_general_dilated(
        field[None],
        taps,
        window_strides=(1, 1),
        padding=((1, 1), (1, 1)),
        lhs_dilation=(2, 2),
        dimension_numbers=("NHWC", "HWIO", "NHWC"),
        preferred_element_type=jnp.float32,
    )[0]


def pointwise_mixing_weights(field, matrix):
    rows, cols, chans = field.shape
    return jnp.dot(
        field.reshape(rows * cols, chans), matrix, preferred_element_type=jnp.float32
    ).reshape(rows, cols, -1)


def project_back(field, matrix):
    rows, cols, chans = field.shape
    out = lax.dot_general(
        field.reshape(rows * cols, chans),
        matrix,
        (((1,), (1,)), ((), ())),
        preferred_element_type=jnp.float32,
    )
    return out.reshape(rows, cols, -1)


def silu_slope(value):
    sig = jax.nn.sigmoid(value)
    return sig * (1.0 + value * (1.0 - sig))


def backward_start(cotangent, central_lifted_mixing):
    back_mid = block_sum(cotangent).astype(jnp.bfloat16)
    grad_mid = project_back(back_mid, central_lifted_mixing)
    return grad_mid, block_sum(grad_mid).astype(jnp.bfloat16)


def shards(
    features,
    station_mask,
    station_gain,
    fine_kernel,
    down_mid,
    mid_kernel,
    down_coarse,
    coarse_kernel,
    up_coarse,
    central_lifted_mixing,
    cotangent,
):
    inputs = (
        features.astype(jnp.float32)
        + station_mask.astype(jnp.float32)[:, :, None] * station_gain[None, None, :]
    ).astype(jnp.bfloat16)
    grad_mid, back_coarse = backward_start(cotangent, central_lifted_mixing)
    in_pad, back_strip = with_halo_and_strip(inputs, back_coarse, 1, 0)
    pre_fine = conv_valid(in_pad, fine_kernel)
    sharpest_level_response = jax.nn.silu(pre_fine).astype(jnp.bfloat16)
    mid_in = pointwise_mixing_weights(pool_mean(sharpest_level_response), down_mid).astype(
        jnp.bfloat16
    )
    pre_mid = conv_valid(with_halo(mid_in, 1), mid_kernel)
    act_mid = jax.nn.silu(pre_mid).astype(jnp.bfloat16)
    x = lax.axis_index("gx")
    nx = lax.axis_size("gx")
    own_chans = coarse_kernel.shape[3]
    own_up = lax.dynamic_slice_in_dim(up_coarse, x * own_chans, own_chans, axis=0)
    pooled_mid = pool_mean(act_mid)
    rows, cols, _ = pooled_mid.shape
    strip = gather_strip(pooled_mid, 2, 2)
    coarse_in = pointwise_mixing_weights(strip, down_coarse).astype(jnp.bfloat16)
    pre_coarse = conv_valid(coarse_in, coarse_kernel, 1)
    act_own = jax.nn.silu(pre_coarse[1 : 1 + rows]).astype(jnp.bfloat16)
    delta_coarse = (
        project_back(back_strip, own_up) * silu_slope(pre_coarse)
    ).astype(jnp.bfloat16)
    into_own = convt_valid(
        delta_coarse, coarse_kernel, 1
    ).astype(jnp.bfloat16)
    down_own = project_back(into_own, down_coarse).astype(jnp.bfloat16)
    blocks = jnp.concatenate([act_own, down_own], axis=2)
    blocks = blocks.reshape(rows, nx, cols, -1).transpose(1, 0, 2, 3).reshape(nx, rows * cols, -1)
    blocks = swap_blocks(blocks, 3)
    act_coarse = blocks[:, :, :own_chans].transpose(1, 0, 2).reshape(rows, cols, nx * own_chans)
    down_back = blocks[:, :, own_chans:].astype(jnp.float32).sum(axis=0).reshape(rows, cols, -1)
    ascend_central_level = (
        up_mix(act_coarse, up_coarse)
        + act_mid.astype(jnp.float32)
    ).astype(jnp.bfloat16)
    predicted_rainfall = (
        up_mix(ascend_central_level, central_lifted_mixing)
        + sharpest_level_response.astype(jnp.float32)
    ).astype(jnp.bfloat16)
    delta_mid = (
        (grad_mid + double_spatial_lattice(down_back) * 0.25)
        * silu_slope(pre_mid)
    ).astype(jnp.bfloat16)
    into_mid = convt_valid(with_halo(delta_mid, 4), mid_kernel).astype(jnp.bfloat16)
    delta_fine = (
        (
            cotangent.astype(jnp.float32)
            + up_mix(into_mid, down_mid.T) * 0.25
        )
        * silu_slope(pre_fine)
    ).astype(jnp.bfloat16)
    local_grad = kernel_grad(in_pad, delta_fine)
    cells_all = features.shape[0] * lax.axis_size("gy") * features.shape[1] * lax.axis_size("gx")
    scale = 1.0 / jnp.sqrt(jnp.float32(cells_all))
    grad_sum, delta_pad = sum_all_with_halo(local_grad, delta_fine, 6)
    sharpest_filter_derivative = grad_sum.astype(jnp.float32) * scale
    hidden_maps_sensitivity = convt_valid(delta_pad, fine_kernel).astype(jnp.bfloat16)
    return (predicted_rainfall, hidden_maps_sensitivity, sharpest_filter_derivative)


def solution(mesh):
    return jax.shard_map(
        shards,
        mesh=mesh,
        in_specs=(
            P("gy", "gx", None),
            P("gy", "gx"),
            P(),
            P(),
            P(),
            P(),
            P(),
            P(None, None, None, "gx"),
            P(),
            P(),
            P("gy", "gx", None),
        ),
        out_specs=(P("gy", "gx", None), P("gy", "gx", None), P()),
        check_vma=False,
    )
```

```python
import functools

import jax
import jax.numpy as jnp
from jax import lax
from jax.experimental import pallas as pl
from jax.experimental.pallas import tpu as pltpu
from jax.sharding import PartitionSpec as P

MESH = pl.DeviceIdType.MESH
VMEM = pl.BlockSpec(memory_space=pltpu.VMEM)

DIRS = ((-1, 0), (1, 0), (0, -1), (0, 1), (-1, -1), (-1, 1), (1, -1), (1, 1))
OPP = (1, 0, 3, 2, 7, 6, 5, 4)


class Halo:
    def __init__(self, ny, nx, x_ref, cols_in, rows, cols, corners, send, recv):
        self.y, self.x = lax.axis_index("gy"), lax.axis_index("gx")
        self.ny, self.nx = ny, nx
        self.x_ref, self.cols_in = x_ref, cols_in
        self.out = (rows, cols, corners)
        self.reach = rows.shape[1]
        self.send, self.recv = send, recv

    def exists(self, d):
        dy, dx = DIRS[d]
        y, x = self.y, self.x
        oky = None if dy == 0 else y > 0 if dy < 0 else y < self.ny - 1
        okx = None if dx == 0 else x > 0 if dx < 0 else x < self.nx - 1
        if oky is None:
            return okx
        return oky if okx is None else jnp.logical_and(oky, okx)

    def device(self, d):
        return (self.y + DIRS[d][0], self.x + DIRS[d][1])

    def source(self, d):
        h, w, _ = self.x_ref.shape
        dy, dx = DIRS[d]
        if d in (2, 3):
            return self.cols_in.at[d - 2]
        r = self.reach
        row = pl.ds(0 if dy < 0 else h - r, r)
        if d < 2:
            return self.x_ref.at[row]
        return self.x_ref.at[row, pl.ds(0 if dx < 0 else w - 16, 16)]

    def slot(self, d):
        rows, cols, corners = self.out
        return rows.at[d] if d < 2 else cols.at[d - 2] if d < 4 else corners.at[d - 4]

    def copy(self, d, slot):
        return pltpu.make_async_remote_copy(
            src_ref=self.source(d),
            dst_ref=self.slot(slot),
            send_sem=self.send.at[d],
            recv_sem=self.recv.at[slot],
            device_id=self.device(d),
            device_id_type=MESH,
        )

    def greet(self, barrier):
        for d in range(8):

            @pl.when(self.exists(d))
            def _(d=d):
                pl.semaphore_signal(
                    barrier, inc=1, device_id=self.device(d), device_id_type=MESH
                )

        above_below = jnp.minimum(self.y, 1) + jnp.minimum(self.ny - 1 - self.y, 1)
        sideways = jnp.minimum(self.x, 1) + jnp.minimum(self.nx - 1 - self.x, 1)
        return (above_below + 1) * (sideways + 1) - 1

    def start(self):
        for d in range(8):

            @pl.when(self.exists(d))
            def _(d=d):
                self.copy(d, OPP[d]).start()

            @pl.when(jnp.logical_not(self.exists(d)))
            def _(d=d):
                slot = self.slot(d)
                slot[...] = jnp.zeros(slot.shape, slot.dtype)

    def wait(self):
        for d in range(8):

            @pl.when(self.exists(d))
            def _(d=d):
                self.copy(d, OPP[d]).wait_send()
                self.copy(d, d).wait_recv()

    def assemble(self, out):
        h, w, _ = self.x_ref.shape
        r, f32 = self.reach, jnp.float32
        rows, cols, corners = self.out

        def edge(i):
            left, right = corners[2 * i].astype(f32), corners[2 * i + 1].astype(f32)
            line = [left[:, 16 - r :], rows[i].astype(f32), right[:, :r]]
            return jnp.concatenate(line, axis=1).astype(out.dtype)

        out[:r] = edge(0)
        out[r + h :] = edge(1)
        left = [cols[0, j].astype(f32)[:, None, :] for j in range(r)]
        right = [cols[1, j].astype(f32)[:, None, :] for j in range(r)]
        middle = left + [self.x_ref[...].astype(f32)] + right
        out[r : r + h] = jnp.concatenate(middle, axis=1).astype(out.dtype)


class Strip:
    def __init__(self, ny, nx, block, out, send, recv):
        self.y, self.x = lax.axis_index("gy"), lax.axis_index("gx")
        self.ny, self.nx = ny, nx
        self.block, self.out, self.send, self.recv = block, out, send, recv
        self.reach = (out.shape[0] - block.shape[0]) // 2
        self.links = strip_links(nx)

    def when(self, dy, run):
        if dy == 0:
            run()
        else:
            pl.when(self.y > 0 if dy < 0 else self.y < self.ny - 1)(run)

    def copy(self, i, slot, device):
        dy, _ = self.links[i]
        h, w, _ = self.block.shape
        r = self.reach
        cols = pl.ds(pl.multiple_of(slot * w, w), w)
        if dy == 0:
            src, dst = self.block, self.out.at[pl.ds(r, h), cols]
        elif dy < 0:
            src, dst = self.block.at[pl.ds(0, r)], self.out.at[pl.ds(r + h, r), cols]
        else:
            src, dst = self.block.at[pl.ds(h - r, r)], self.out.at[pl.ds(0, r), cols]
        return pltpu.make_async_remote_copy(
            src_ref=src,
            dst_ref=dst,
            send_sem=self.send.at[i],
            recv_sem=self.recv.at[i],
            device_id=device,
            device_id_type=MESH,
        )

    def target(self, i):
        dy, k = self.links[i]
        return (self.y + dy, lax.rem(self.x + k, self.nx))

    def origin(self, i):
        dy, k = self.links[i]
        return (self.y - dy, lax.rem(self.x - k + self.nx, self.nx))

    def greet(self, barrier):
        for i, (dy, _) in enumerate(self.links):

            def signal(i=i):
                pl.semaphore_signal(
                    barrier, inc=1, device_id=self.target(i), device_id_type=MESH
                )

            self.when(dy, signal)
        above_below = jnp.minimum(self.y, 1) + jnp.minimum(self.ny - 1 - self.y, 1)
        return self.nx - 1 + above_below * self.nx

    def start(self):
        for i, (dy, _) in enumerate(self.links):
            self.when(dy, lambda i=i: self.copy(i, self.x, self.target(i)).start())
        h, w, c = self.block.shape
        r = self.reach
        cols = pl.ds(pl.multiple_of(self.x * w, w), w)
        self.out[r : r + h, cols, :] = self.block[...]
        rim = jnp.zeros((r, self.nx * w, c), self.out.dtype)

        @pl.when(self.y == 0)
        def _():
            self.out[:r] = rim

        @pl.when(self.y == self.ny - 1)
        def _():
            self.out[r + h :] = rim

    def wait(self):
        for i, (dy, _) in enumerate(self.links):
            self.when(dy, lambda i=i: self.copy(i, self.x, self.target(i)).wait_send())
            self.when(
                -dy, lambda i=i: self.copy(i, self.origin(i)[1], self.origin(i)).wait_recv()
            )


def strip_links(nx):
    return [(0, k) for k in range(1, nx)] + [(dy, k) for dy in (-1, 1) for k in range(nx)]


def strip_sems(nx):
    return [pltpu.SemaphoreType.DMA((len(strip_links(nx)),))] * 2


def strip_shape(block, reach, nx):
    h, w, c = block.shape
    return jax.ShapeDtypeStruct((h + 2 * reach, w * nx, c), block.dtype)


def halo_scratch(x, r=1):
    h, w, c = x.shape
    shapes = [(2, r, w, c), (2, r, h, c), (4, r, 16, c)]
    return [pltpu.VMEM(a, x.dtype) for a in shapes] + [pltpu.SemaphoreType.DMA((8,))] * 2


def halo_shape(x, r=1):
    h, w, c = x.shape
    return jax.ShapeDtypeStruct((h + 2 * r, w + 2 * r, c), x.dtype)


def halo_cols(x, r=1):
    h, w, c = x.shape
    both = jnp.concatenate([x[:, :r], x[:, w - r :]], axis=1)
    return both.transpose(1, 0, 2).reshape(2, r, h, c)


def halo_kernel(ny, nx, field, cols_in, out, *scratch):
    halo = Halo(ny, nx, field, cols_in, *scratch)
    barrier = pltpu.get_barrier_semaphore()
    pl.semaphore_wait(barrier, halo.greet(barrier))
    halo.start()
    halo.wait()
    halo.assemble(out)


def with_halo(x, call_id):
    ny, nx = lax.axis_size("gy"), lax.axis_size("gx")
    return pl.pallas_call(
        functools.partial(halo_kernel, ny, nx),
        out_shape=halo_shape(x),
        in_specs=[VMEM] * 2,
        out_specs=VMEM,
        scratch_shapes=halo_scratch(x),
        compiler_params=pltpu.CompilerParams(collective_id=call_id, has_side_effects=True),
        name="halo",
    )(x, halo_cols(x))


def first_kernel(ny, nx, field, cols_in, block, out, strip_out, *scratch):
    halo = Halo(ny, nx, field, cols_in, *scratch[:5])
    strip = Strip(ny, nx, block, strip_out, *scratch[5:])
    barrier = pltpu.get_barrier_semaphore()
    pl.semaphore_wait(barrier, halo.greet(barrier) + strip.greet(barrier))
    halo.start()
    strip.start()
    halo.wait()
    halo.assemble(out)
    strip.wait()


def with_halo_and_strip(x, rim, block, reach, call_id):
    ny, nx = lax.axis_size("gy"), lax.axis_size("gx")
    return pl.pallas_call(
        functools.partial(first_kernel, ny, nx),
        out_shape=[halo_shape(x, rim), strip_shape(block, reach, nx)],
        in_specs=[VMEM] * 3,
        out_specs=[VMEM] * 2,
        scratch_shapes=halo_scratch(x, rim) + strip_sems(nx),
        compiler_params=pltpu.CompilerParams(collective_id=call_id, has_side_effects=True),
        name="halo_strip",
    )(x, halo_cols(x, rim), block)


def strip_kernel(ny, nx, block, out, send, recv):
    strip = Strip(ny, nx, block, out, send, recv)
    barrier = pltpu.get_barrier_semaphore()
    pl.semaphore_wait(barrier, strip.greet(barrier))
    strip.start()
    strip.wait()


def gather_strip(block, reach, call_id):
    ny, nx = lax.axis_size("gy"), lax.axis_size("gx")
    return pl.pallas_call(
        functools.partial(strip_kernel, ny, nx),
        out_shape=strip_shape(block, reach, nx),
        in_specs=[VMEM],
        out_specs=VMEM,
        scratch_shapes=strip_sems(nx),
        compiler_params=pltpu.CompilerParams(collective_id=call_id, has_side_effects=True),
        name="strip",
    )(block)


def swap_kernel(nx, blocks, out, send, recv):
    y, x = lax.axis_index("gy"), lax.axis_index("gx")

    def copy(k, src_slot, dst_slot, device):
        return pltpu.make_async_remote_copy(
            src_ref=blocks.at[src_slot],
            dst_ref=out.at[dst_slot],
            send_sem=send.at[k],
            recv_sem=recv.at[k],
            device_id=(y, device),
            device_id_type=MESH,
        )

    barrier = pltpu.get_barrier_semaphore()
    for k in range(1, nx):
        pl.semaphore_signal(
            barrier, inc=1, device_id=(y, lax.rem(x + k, nx)), device_id_type=MESH
        )
    pl.semaphore_wait(barrier, nx - 1)
    for k in range(1, nx):
        to = lax.rem(x + k, nx)
        copy(k, to, x, to).start()
    out[x] = blocks[x]
    for k in range(1, nx):
        to = lax.rem(x + k, nx)
        source = lax.rem(x - k + nx, nx)
        copy(k, to, x, to).wait_send()
        copy(k, to, source, source).wait_recv()


def swap_blocks(blocks, call_id):
    nx = lax.axis_size("gx")
    return pl.pallas_call(
        functools.partial(swap_kernel, nx),
        out_shape=jax.ShapeDtypeStruct(blocks.shape, blocks.dtype),
        in_specs=[VMEM],
        out_specs=VMEM,
        scratch_shapes=[pltpu.SemaphoreType.DMA((nx,)), pltpu.SemaphoreType.DMA((nx,))],
        compiler_params=pltpu.CompilerParams(collective_id=call_id, has_side_effects=True),
        name="swap",
    )(blocks)


def sum_kernel(ny, nx, src, field, cols_in, out, field_out, got_y, got_x, *scratch):
    s1, r1, s2, r2, s3, r3 = scratch[:6]
    y, x = lax.axis_index("gy"), lax.axis_index("gx")
    f32 = jnp.float32
    halo = Halo(ny, nx, field, cols_in, *scratch[6:])

    def copy(a, b, s, r, device):
        return pltpu.make_async_remote_copy(
            src_ref=a, dst_ref=b, send_sem=s, recv_sem=r, device_id=device, device_id_type=MESH
        )

    def over_y(k):
        return (lax.rem(y + k, ny), x)

    def over_x(k):
        return (y, lax.rem(x + k, nx))

    barrier = pltpu.get_barrier_semaphore()
    for k in range(1, ny):
        pl.semaphore_signal(barrier, inc=1, device_id=over_y(k), device_id_type=MESH)
    for k in range(1, nx):
        pl.semaphore_signal(barrier, inc=1, device_id=over_x(k), device_id_type=MESH)
    pl.semaphore_wait(barrier, halo.greet(barrier) + ny + nx - 2)
    halo.start()

    for k in range(1, ny):
        to = over_y(k)
        copy(src.at[to[0]], got_y.at[k], s1.at[k], r1.at[k], to).start()
    total = src[y].astype(f32)
    for k in range(1, ny):
        to = over_y(k)
        copy(src.at[to[0]], got_y.at[k], s1.at[k], r1.at[k], to).wait()
        total = total + got_y[k].astype(f32)
    got_x[x] = total.astype(got_x.dtype)

    for k in range(1, nx):
        copy(got_x.at[x], got_x.at[x], s2.at[k], r2.at[k], over_x(k)).start()
    halo.wait()
    halo.assemble(field_out)
    for k in range(1, nx):
        source = lax.rem(x - k + nx, nx)
        copy(got_x.at[x], got_x.at[x], s2.at[k], r2.at[k], over_x(k)).wait_send()
        copy(got_x.at[x], got_x.at[source], s2.at[k], r2.at[k], over_x(k)).wait_recv()
    total = got_x[0].astype(f32)
    for p in range(1, nx):
        total = total + got_x[p].astype(f32)
    out[y] = total.astype(out.dtype)

    for k in range(1, ny):
        copy(out.at[y], out.at[y], s3.at[k], r3.at[k], over_y(k)).start()
    for k in range(1, ny):
        source = lax.rem(y - k + ny, ny)
        copy(out.at[y], out.at[y], s3.at[k], r3.at[k], over_y(k)).wait_send()
        copy(out.at[y], out.at[source], s3.at[k], r3.at[k], over_y(k)).wait_recv()


def sum_all_with_halo(term, field, call_id):
    ny, nx = lax.axis_size("gy"), lax.axis_size("gx")
    lanes = term.shape[-1]
    flat = term.reshape(-1, lanes)
    part = -(-flat.shape[0] // ny)
    part = -(-part // 16) * 16
    padded = jnp.pad(flat.astype(jnp.bfloat16), ((0, part * ny - flat.shape[0]), (0, 0)))
    blocks = padded.reshape(ny, part, lanes)
    dma = pltpu.SemaphoreType.DMA
    total, padded_field = pl.pallas_call(
        functools.partial(sum_kernel, ny, nx),
        out_shape=[jax.ShapeDtypeStruct(blocks.shape, blocks.dtype), halo_shape(field)],
        in_specs=[VMEM] * 3,
        out_specs=[VMEM] * 2,
        scratch_shapes=[
            pltpu.VMEM((ny, part, lanes), jnp.bfloat16),
            pltpu.VMEM((nx, part, lanes), jnp.bfloat16),
            dma((ny,)),
            dma((ny,)),
            dma((nx,)),
            dma((nx,)),
            dma((ny,)),
            dma((ny,)),
        ]
        + halo_scratch(field),
        compiler_params=pltpu.CompilerParams(collective_id=call_id, has_side_effects=True),
        name="sum_all",
    )(blocks, field, halo_cols(field))
    total = total.reshape(ny * part, lanes)[: flat.shape[0]].reshape(term.shape)
    return total, padded_field


def conv_valid(padded, kernel, side=0):
    return lax.conv_general_dilated(
        padded[None],
        kernel,
        window_strides=(1, 1),
        padding=((0, 0), (side, side)),
        dimension_numbers=("NHWC", "HWIO", "NHWC"),
        preferred_element_type=jnp.float32,
    )[0]


def convt_valid(padded, kernel, side=0):
    return lax.conv_general_dilated(
        padded[None],
        kernel[::-1, ::-1],
        window_strides=(1, 1),
        padding=((0, 0), (side, side)),
        dimension_numbers=("NHWC", "HWOI", "NHWC"),
        preferred_element_type=jnp.float32,
    )[0]


def kernel_grad(padded, delta):
    rows = padded.shape[0] - 2
    cols = padded.shape[1] - 2
    flat_delta = delta.reshape(rows * cols, -1)
    blocks = []
    for row_off in range(3):
        line = []
        for col_off in range(3):
            window = padded[row_off : row_off + rows, col_off : col_off + cols].reshape(
                rows * cols, -1
            )
            line.append(
                lax.dot_general(
                    window, flat_delta, (((0,), (0,)), ((), ())), preferred_element_type=jnp.float32
                )
            )
        blocks.append(jnp.stack(line))
    return jnp.stack(blocks)


def pool_mean(field):
    rows, cols, chans = field.shape
    return (
        field.astype(jnp.float32)
        .reshape(rows // 2, 2, cols // 2, 2, chans)
        .mean(axis=(1, 3))
        .astype(jnp.bfloat16)
    )


def block_sum(field):
    rows, cols, chans = field.shape
    return field.astype(jnp.float32).reshape(rows // 2, 2, cols // 2, 2, chans).sum(axis=(1, 3))


def double_spatial_lattice(field):
    return jnp.repeat(jnp.repeat(field, 2, axis=0), 2, axis=1)


def up_mix(field, matrix):
    taps = jnp.broadcast_to(matrix, (2, 2) + matrix.shape)
    return lax.conv_general_dilated(
        field[None],
        taps,
        window_strides=(1, 1),
        padding=((1, 1), (1, 1)),
        lhs_dilation=(2, 2),
        dimension_numbers=("NHWC", "HWIO", "NHWC"),
        preferred_element_type=jnp.float32,
    )[0]


def pointwise_mixing_weights(field, matrix):
    rows, cols, chans = field.shape
    return jnp.dot(
        field.reshape(rows * cols, chans), matrix, preferred_element_type=jnp.float32
    ).reshape(rows, cols, -1)


def project_back(field, matrix):
    rows, cols, chans = field.shape
    out = lax.dot_general(
        field.reshape(rows * cols, chans),
        matrix,
        (((1,), (1,)), ((), ())),
        preferred_element_type=jnp.float32,
    )
    return out.reshape(rows, cols, -1)


def silu_slope(value):
    sig = jax.nn.sigmoid(value)
    return sig * (1.0 + value * (1.0 - sig))


def inside(padded):
    ok = []
    for axis, dim in (("gy", 0), ("gx", 1)):
        length = padded.shape[dim] - 2
        place = lax.axis_index(axis) * length - 1 + jnp.arange(length + 2)
        ok.append((place >= 0) & (place < length * lax.axis_size(axis)))
    return (ok[0][:, None] & ok[1][None, :])[:, :, None]


def backward_start(cotangent, central_lifted_mixing):
    back_mid = block_sum(cotangent).astype(jnp.bfloat16)
    grad_mid = project_back(back_mid, central_lifted_mixing)
    return grad_mid, block_sum(grad_mid).astype(jnp.bfloat16)


def shards(
    features,
    station_mask,
    station_gain,
    fine_kernel,
    down_mid,
    mid_kernel,
    down_coarse,
    coarse_kernel,
    up_coarse,
    central_lifted_mixing,
    cotangent,
):
    inputs = (
        features.astype(jnp.float32)
        + station_mask.astype(jnp.float32)[:, :, None] * station_gain[None, None, :]
    ).astype(jnp.bfloat16)
    grad_mid, back_coarse = backward_start(cotangent, central_lifted_mixing)
    wide, back_strip = with_halo_and_strip(inputs, 3, back_coarse, 1, 0)
    in_pad = wide[2:-2, 2:-2]
    pre_wide = conv_valid(wide, fine_kernel)
    pre_fine = pre_wide[2:-2, 2:-2]
    act_wide = jax.nn.silu(pre_wide).astype(jnp.bfloat16)
    sharpest_level_response = act_wide[2:-2, 2:-2]
    mid_in = pointwise_mixing_weights(pool_mean(act_wide), down_mid).astype(
        jnp.bfloat16
    )
    pre_mid = conv_valid(jnp.where(inside(mid_in), mid_in, jnp.zeros((), mid_in.dtype)), mid_kernel)
    act_mid = jax.nn.silu(pre_mid).astype(jnp.bfloat16)
    x = lax.axis_index("gx")
    nx = lax.axis_size("gx")
    own_chans = coarse_kernel.shape[3]
    own_up = lax.dynamic_slice_in_dim(up_coarse, x * own_chans, own_chans, axis=0)
    pooled_mid = pool_mean(act_mid)
    rows, cols, _ = pooled_mid.shape
    strip = gather_strip(pooled_mid, 2, 2)
    coarse_in = pointwise_mixing_weights(strip, down_coarse).astype(jnp.bfloat16)
    pre_coarse = conv_valid(coarse_in, coarse_kernel, 1)
    act_own = jax.nn.silu(pre_coarse[1 : 1 + rows]).astype(jnp.bfloat16)
    delta_coarse = (
        project_back(back_strip, own_up) * silu_slope(pre_coarse)
    ).astype(jnp.bfloat16)
    into_own = convt_valid(
        delta_coarse, coarse_kernel, 1
    ).astype(jnp.bfloat16)
    down_own = project_back(into_own, down_coarse).astype(jnp.bfloat16)
    blocks = jnp.concatenate([act_own, down_own], axis=2)
    blocks = blocks.reshape(rows, nx, cols, -1).transpose(1, 0, 2, 3).reshape(nx, rows * cols, -1)
    blocks = swap_blocks(blocks, 3)
    act_coarse = blocks[:, :, :own_chans].transpose(1, 0, 2).reshape(rows, cols, nx * own_chans)
    down_back = blocks[:, :, own_chans:].astype(jnp.float32).sum(axis=0).reshape(rows, cols, -1)
    ascend_central_level = (
        up_mix(act_coarse, up_coarse)
        + act_mid.astype(jnp.float32)
    ).astype(jnp.bfloat16)
    predicted_rainfall = (
        up_mix(ascend_central_level, central_lifted_mixing)
        + sharpest_level_response.astype(jnp.float32)
    ).astype(jnp.bfloat16)
    delta_mid = (
        (grad_mid + double_spatial_lattice(down_back) * 0.25)
        * silu_slope(pre_mid)
    ).astype(jnp.bfloat16)
    into_mid = convt_valid(with_halo(delta_mid, 4), mid_kernel).astype(jnp.bfloat16)
    delta_fine = (
        (
            cotangent.astype(jnp.float32)
            + up_mix(into_mid, down_mid.T) * 0.25
        )
        * silu_slope(pre_fine)
    ).astype(jnp.bfloat16)
    local_grad = kernel_grad(in_pad, delta_fine)
    cells_all = features.shape[0] * lax.axis_size("gy") * features.shape[1] * lax.axis_size("gx")
    scale = 1.0 / jnp.sqrt(jnp.float32(cells_all))
    grad_sum, delta_pad = sum_all_with_halo(local_grad, delta_fine, 6)
    sharpest_filter_derivative = grad_sum.astype(jnp.float32) * scale
    hidden_maps_sensitivity = convt_valid(delta_pad, fine_kernel).astype(jnp.bfloat16)
    return (predicted_rainfall, hidden_maps_sensitivity, sharpest_filter_derivative)


def solution(mesh):
    return jax.shard_map(
        shards,
        mesh=mesh,
        in_specs=(
            P("gy", "gx", None),
            P("gy", "gx"),
            P(),
            P(),
            P(),
            P(),
            P(),
            P(None, None, None, "gx"),
            P(),
            P(),
            P("gy", "gx", None),
        ),
        out_specs=(P("gy", "gx", None), P("gy", "gx", None), P()),
        check_vma=False,
    )
```

```python
import functools

import jax
import jax.numpy as jnp
from jax import lax
from jax.experimental import pallas as pl
from jax.experimental.pallas import tpu as pltpu
from jax.sharding import PartitionSpec as P

MESH = pl.DeviceIdType.MESH
VMEM = pl.BlockSpec(memory_space=pltpu.VMEM)

DIRS = ((-1, 0), (1, 0), (0, -1), (0, 1), (-1, -1), (-1, 1), (1, -1), (1, 1))
OPP = (1, 0, 3, 2, 7, 6, 5, 4)


class Halo:
    def __init__(self, ny, nx, x_ref, cols_in, rows, cols, corners, send, recv):
        self.y, self.x = lax.axis_index("gy"), lax.axis_index("gx")
        self.ny, self.nx = ny, nx
        self.x_ref, self.cols_in = x_ref, cols_in
        self.out = (rows, cols, corners)
        self.reach = rows.shape[1]
        self.send, self.recv = send, recv

    def exists(self, d):
        dy, dx = DIRS[d]
        y, x = self.y, self.x
        oky = None if dy == 0 else y > 0 if dy < 0 else y < self.ny - 1
        okx = None if dx == 0 else x > 0 if dx < 0 else x < self.nx - 1
        if oky is None:
            return okx
        return oky if okx is None else jnp.logical_and(oky, okx)

    def device(self, d):
        return (self.y + DIRS[d][0], self.x + DIRS[d][1])

    def source(self, d):
        h, w, _ = self.x_ref.shape
        dy, dx = DIRS[d]
        if d in (2, 3):
            return self.cols_in.at[d - 2]
        r = self.reach
        row = pl.ds(0 if dy < 0 else h - r, r)
        if d < 2:
            return self.x_ref.at[row]
        return self.x_ref.at[row, pl.ds(0 if dx < 0 else w - 16, 16)]

    def slot(self, d):
        rows, cols, corners = self.out
        return rows.at[d] if d < 2 else cols.at[d - 2] if d < 4 else corners.at[d - 4]

    def copy(self, d, slot):
        return pltpu.make_async_remote_copy(
            src_ref=self.source(d),
            dst_ref=self.slot(slot),
            send_sem=self.send.at[d],
            recv_sem=self.recv.at[slot],
            device_id=self.device(d),
            device_id_type=MESH,
        )

    def greet(self, barrier):
        for d in range(8):

            @pl.when(self.exists(d))
            def _(d=d):
                pl.semaphore_signal(
                    barrier, inc=1, device_id=self.device(d), device_id_type=MESH
                )

        above_below = jnp.minimum(self.y, 1) + jnp.minimum(self.ny - 1 - self.y, 1)
        sideways = jnp.minimum(self.x, 1) + jnp.minimum(self.nx - 1 - self.x, 1)
        return (above_below + 1) * (sideways + 1) - 1

    def start(self):
        for d in range(8):

            @pl.when(self.exists(d))
            def _(d=d):
                self.copy(d, OPP[d]).start()

            @pl.when(jnp.logical_not(self.exists(d)))
            def _(d=d):
                slot = self.slot(d)
                slot[...] = jnp.zeros(slot.shape, slot.dtype)

    def wait(self):
        for d in range(8):

            @pl.when(self.exists(d))
            def _(d=d):
                self.copy(d, OPP[d]).wait_send()
                self.copy(d, d).wait_recv()

    def assemble(self, out):
        h, w, _ = self.x_ref.shape
        r, f32 = self.reach, jnp.float32
        rows, cols, corners = self.out

        def edge(i):
            left, right = corners[2 * i].astype(f32), corners[2 * i + 1].astype(f32)
            line = [left[:, 16 - r :], rows[i].astype(f32), right[:, :r]]
            return jnp.concatenate(line, axis=1).astype(out.dtype)

        out[:r] = edge(0)
        out[r + h :] = edge(1)
        left = [cols[0, j].astype(f32)[:, None, :] for j in range(r)]
        right = [cols[1, j].astype(f32)[:, None, :] for j in range(r)]
        middle = left + [self.x_ref[...].astype(f32)] + right
        out[r : r + h] = jnp.concatenate(middle, axis=1).astype(out.dtype)


class Strip:
    def __init__(self, ny, nx, block, out, send, recv):
        self.y, self.x = lax.axis_index("gy"), lax.axis_index("gx")
        self.ny, self.nx = ny, nx
        self.block, self.out, self.send, self.recv = block, out, send, recv
        self.reach = (out.shape[0] - block.shape[0]) // 2
        self.links = strip_links(nx)

    def when(self, dy, run):
        if dy == 0:
            run()
        else:
            pl.when(self.y > 0 if dy < 0 else self.y < self.ny - 1)(run)

    def copy(self, i, slot, device):
        dy, _ = self.links[i]
        h, w, _ = self.block.shape
        r = self.reach
        cols = pl.ds(pl.multiple_of(slot * w, w), w)
        if dy == 0:
            src, dst = self.block, self.out.at[pl.ds(r, h), cols]
        elif dy < 0:
            src, dst = self.block.at[pl.ds(0, r)], self.out.at[pl.ds(r + h, r), cols]
        else:
            src, dst = self.block.at[pl.ds(h - r, r)], self.out.at[pl.ds(0, r), cols]
        return pltpu.make_async_remote_copy(
            src_ref=src,
            dst_ref=dst,
            send_sem=self.send.at[i],
            recv_sem=self.recv.at[i],
            device_id=device,
            device_id_type=MESH,
        )

    def target(self, i):
        dy, k = self.links[i]
        return (self.y + dy, lax.rem(self.x + k, self.nx))

    def origin(self, i):
        dy, k = self.links[i]
        return (self.y - dy, lax.rem(self.x - k + self.nx, self.nx))

    def greet(self, barrier):
        for i, (dy, _) in enumerate(self.links):

            def signal(i=i):
                pl.semaphore_signal(
                    barrier, inc=1, device_id=self.target(i), device_id_type=MESH
                )

            self.when(dy, signal)
        above_below = jnp.minimum(self.y, 1) + jnp.minimum(self.ny - 1 - self.y, 1)
        return self.nx - 1 + above_below * self.nx

    def start(self):
        for i, (dy, _) in enumerate(self.links):
            self.when(dy, lambda i=i: self.copy(i, self.x, self.target(i)).start())
        h, w, c = self.block.shape
        r = self.reach
        cols = pl.ds(pl.multiple_of(self.x * w, w), w)
        self.out[r : r + h, cols, :] = self.block[...]
        rim = jnp.zeros((r, self.nx * w, c), self.out.dtype)

        @pl.when(self.y == 0)
        def _():
            self.out[:r] = rim

        @pl.when(self.y == self.ny - 1)
        def _():
            self.out[r + h :] = rim

    def wait(self):
        for i, (dy, _) in enumerate(self.links):
            self.when(dy, lambda i=i: self.copy(i, self.x, self.target(i)).wait_send())
            self.when(
                -dy, lambda i=i: self.copy(i, self.origin(i)[1], self.origin(i)).wait_recv()
            )


def strip_links(nx):
    return [(0, k) for k in range(1, nx)] + [(dy, k) for dy in (-1, 1) for k in range(nx)]


def strip_sems(nx):
    return [pltpu.SemaphoreType.DMA((len(strip_links(nx)),))] * 2


def strip_shape(block, reach, nx):
    h, w, c = block.shape
    return jax.ShapeDtypeStruct((h + 2 * reach, w * nx, c), block.dtype)


def halo_scratch(x, r=1):
    h, w, c = x.shape
    shapes = [(2, r, w, c), (2, r, h, c), (4, r, 16, c)]
    return [pltpu.VMEM(a, x.dtype) for a in shapes] + [pltpu.SemaphoreType.DMA((8,))] * 2


def halo_shape(x, r=1):
    h, w, c = x.shape
    return jax.ShapeDtypeStruct((h + 2 * r, w + 2 * r, c), x.dtype)


def halo_cols(x, r=1):
    h, w, c = x.shape
    both = jnp.concatenate([x[:, :r], x[:, w - r :]], axis=1)
    return both.transpose(1, 0, 2).reshape(2, r, h, c)


def halo_kernel(ny, nx, field, cols_in, out, *scratch):
    halo = Halo(ny, nx, field, cols_in, *scratch)
    barrier = pltpu.get_barrier_semaphore()
    pl.semaphore_wait(barrier, halo.greet(barrier))
    halo.start()
    halo.wait()
    halo.assemble(out)


def with_halo(x, call_id):
    ny, nx = lax.axis_size("gy"), lax.axis_size("gx")
    return pl.pallas_call(
        functools.partial(halo_kernel, ny, nx),
        out_shape=halo_shape(x),
        in_specs=[VMEM] * 2,
        out_specs=VMEM,
        scratch_shapes=halo_scratch(x),
        compiler_params=pltpu.CompilerParams(collective_id=call_id, has_side_effects=True),
        name="halo",
    )(x, halo_cols(x))


def first_kernel(ny, nx, field, cols_in, block, out, strip_out, *scratch):
    halo = Halo(ny, nx, field, cols_in, *scratch[:5])
    strip = Strip(ny, nx, block, strip_out, *scratch[5:])
    barrier = pltpu.get_barrier_semaphore()
    pl.semaphore_wait(barrier, halo.greet(barrier) + strip.greet(barrier))
    halo.start()
    strip.start()
    halo.wait()
    halo.assemble(out)
    strip.wait()


def with_halo_and_strip(x, rim, block, reach, call_id):
    ny, nx = lax.axis_size("gy"), lax.axis_size("gx")
    return pl.pallas_call(
        functools.partial(first_kernel, ny, nx),
        out_shape=[halo_shape(x, rim), strip_shape(block, reach, nx)],
        in_specs=[VMEM] * 3,
        out_specs=[VMEM] * 2,
        scratch_shapes=halo_scratch(x, rim) + strip_sems(nx),
        compiler_params=pltpu.CompilerParams(collective_id=call_id, has_side_effects=True),
        name="halo_strip",
    )(x, halo_cols(x, rim), block)


def strip_kernel(ny, nx, block, out, send, recv):
    strip = Strip(ny, nx, block, out, send, recv)
    barrier = pltpu.get_barrier_semaphore()
    pl.semaphore_wait(barrier, strip.greet(barrier))
    strip.start()
    strip.wait()


def gather_strip(block, reach, call_id):
    ny, nx = lax.axis_size("gy"), lax.axis_size("gx")
    return pl.pallas_call(
        functools.partial(strip_kernel, ny, nx),
        out_shape=strip_shape(block, reach, nx),
        in_specs=[VMEM],
        out_specs=VMEM,
        scratch_shapes=strip_sems(nx),
        compiler_params=pltpu.CompilerParams(collective_id=call_id, has_side_effects=True),
        name="strip",
    )(block)


def swap_kernel(nx, blocks, out, send, recv):
    y, x = lax.axis_index("gy"), lax.axis_index("gx")

    def copy(k, src_slot, dst_slot, device):
        return pltpu.make_async_remote_copy(
            src_ref=blocks.at[src_slot],
            dst_ref=out.at[dst_slot],
            send_sem=send.at[k],
            recv_sem=recv.at[k],
            device_id=(y, device),
            device_id_type=MESH,
        )

    barrier = pltpu.get_barrier_semaphore()
    for k in range(1, nx):
        pl.semaphore_signal(
            barrier, inc=1, device_id=(y, lax.rem(x + k, nx)), device_id_type=MESH
        )
    pl.semaphore_wait(barrier, nx - 1)
    for k in range(1, nx):
        to = lax.rem(x + k, nx)
        copy(k, to, x, to).start()
    out[x] = blocks[x]
    for k in range(1, nx):
        to = lax.rem(x + k, nx)
        source = lax.rem(x - k + nx, nx)
        copy(k, to, x, to).wait_send()
        copy(k, to, source, source).wait_recv()


def swap_blocks(blocks, call_id):
    nx = lax.axis_size("gx")
    return pl.pallas_call(
        functools.partial(swap_kernel, nx),
        out_shape=jax.ShapeDtypeStruct(blocks.shape, blocks.dtype),
        in_specs=[VMEM],
        out_specs=VMEM,
        scratch_shapes=[pltpu.SemaphoreType.DMA((nx,)), pltpu.SemaphoreType.DMA((nx,))],
        compiler_params=pltpu.CompilerParams(collective_id=call_id, has_side_effects=True),
        name="swap",
    )(blocks)


def sum_kernel(
    ny, nx, src, field, cols_in, blocks, out, field_out, blocks_out, got_y, got_x, *scratch
):
    s1, r1, s2, r2, s3, r3, s4, r4 = scratch[:8]
    y, x = lax.axis_index("gy"), lax.axis_index("gx")
    f32 = jnp.float32
    halo = Halo(ny, nx, field, cols_in, *scratch[8:])

    def copy(a, b, s, r, device):
        return pltpu.make_async_remote_copy(
            src_ref=a, dst_ref=b, send_sem=s, recv_sem=r, device_id=device, device_id_type=MESH
        )

    def over_y(k):
        return (lax.rem(y + k, ny), x)

    def over_x(k):
        return (y, lax.rem(x + k, nx))

    barrier = pltpu.get_barrier_semaphore()
    for k in range(1, ny):
        pl.semaphore_signal(barrier, inc=1, device_id=over_y(k), device_id_type=MESH)
    for k in range(1, nx):
        pl.semaphore_signal(barrier, inc=1, device_id=over_x(k), device_id_type=MESH)
    pl.semaphore_wait(barrier, halo.greet(barrier) + ny + nx - 2)
    halo.start()
    for k in range(1, nx):
        to = over_x(k)
        copy(blocks.at[to[1]], blocks_out.at[x], s4.at[k], r4.at[k], to).start()
    blocks_out[x] = blocks[x]

    for k in range(1, ny):
        to = over_y(k)
        copy(src.at[to[0]], got_y.at[k], s1.at[k], r1.at[k], to).start()
    total = src[y].astype(f32)
    for k in range(1, ny):
        to = over_y(k)
        copy(src.at[to[0]], got_y.at[k], s1.at[k], r1.at[k], to).wait()
        total = total + got_y[k].astype(f32)
    got_x[x] = total.astype(got_x.dtype)

    for k in range(1, nx):
        copy(got_x.at[x], got_x.at[x], s2.at[k], r2.at[k], over_x(k)).start()
    halo.wait()
    halo.assemble(field_out)
    for k in range(1, nx):
        source = lax.rem(x - k + nx, nx)
        copy(got_x.at[x], got_x.at[x], s2.at[k], r2.at[k], over_x(k)).wait_send()
        copy(got_x.at[x], got_x.at[source], s2.at[k], r2.at[k], over_x(k)).wait_recv()
    total = got_x[0].astype(f32)
    for p in range(1, nx):
        total = total + got_x[p].astype(f32)
    out[y] = total.astype(out.dtype)

    for k in range(1, ny):
        copy(out.at[y], out.at[y], s3.at[k], r3.at[k], over_y(k)).start()
    for k in range(1, ny):
        source = lax.rem(y - k + ny, ny)
        copy(out.at[y], out.at[y], s3.at[k], r3.at[k], over_y(k)).wait_send()
        copy(out.at[y], out.at[source], s3.at[k], r3.at[k], over_y(k)).wait_recv()
    for k in range(1, nx):
        to = over_x(k)
        source = lax.rem(x - k + nx, nx)
        copy(blocks.at[to[1]], blocks_out.at[x], s4.at[k], r4.at[k], to).wait_send()
        copy(blocks.at[to[1]], blocks_out.at[source], s4.at[k], r4.at[k], to).wait_recv()


def sum_all_with_halo(term, field, swapped, call_id):
    ny, nx = lax.axis_size("gy"), lax.axis_size("gx")
    lanes = term.shape[-1]
    flat = term.reshape(-1, lanes)
    part = -(-flat.shape[0] // ny)
    part = -(-part // 16) * 16
    padded = jnp.pad(flat.astype(jnp.bfloat16), ((0, part * ny - flat.shape[0]), (0, 0)))
    blocks = padded.reshape(ny, part, lanes)
    dma = pltpu.SemaphoreType.DMA
    total, padded_field, swapped = pl.pallas_call(
        functools.partial(sum_kernel, ny, nx),
        out_shape=[
            jax.ShapeDtypeStruct(blocks.shape, blocks.dtype),
            halo_shape(field),
            jax.ShapeDtypeStruct(swapped.shape, swapped.dtype),
        ],
        in_specs=[VMEM] * 4,
        out_specs=[VMEM] * 3,
        scratch_shapes=[
            pltpu.VMEM((ny, part, lanes), jnp.bfloat16),
            pltpu.VMEM((nx, part, lanes), jnp.bfloat16),
            dma((ny,)),
            dma((ny,)),
            dma((nx,)),
            dma((nx,)),
            dma((ny,)),
            dma((ny,)),
            dma((nx,)),
            dma((nx,)),
        ]
        + halo_scratch(field),
        compiler_params=pltpu.CompilerParams(collective_id=call_id, has_side_effects=True),
        name="sum_all",
    )(blocks, field, halo_cols(field), swapped)
    total = total.reshape(ny * part, lanes)[: flat.shape[0]].reshape(term.shape)
    return total, padded_field, swapped


def conv_valid(padded, kernel, side=0):
    return lax.conv_general_dilated(
        padded[None],
        kernel,
        window_strides=(1, 1),
        padding=((0, 0), (side, side)),
        dimension_numbers=("NHWC", "HWIO", "NHWC"),
        preferred_element_type=jnp.float32,
    )[0]


def convt_valid(padded, kernel, side=0):
    return lax.conv_general_dilated(
        padded[None],
        kernel[::-1, ::-1],
        window_strides=(1, 1),
        padding=((0, 0), (side, side)),
        dimension_numbers=("NHWC", "HWOI", "NHWC"),
        preferred_element_type=jnp.float32,
    )[0]


def kernel_grad(padded, delta):
    rows = padded.shape[0] - 2
    cols = padded.shape[1] - 2
    flat_delta = delta.reshape(rows * cols, -1)
    blocks = []
    for row_off in range(3):
        line = []
        for col_off in range(3):
            window = padded[row_off : row_off + rows, col_off : col_off + cols].reshape(
                rows * cols, -1
            )
            line.append(
                lax.dot_general(
                    window, flat_delta, (((0,), (0,)), ((), ())), preferred_element_type=jnp.float32
                )
            )
        blocks.append(jnp.stack(line))
    return jnp.stack(blocks)


def pool_mean(field):
    rows, cols, chans = field.shape
    return (
        field.astype(jnp.float32)
        .reshape(rows // 2, 2, cols // 2, 2, chans)
        .mean(axis=(1, 3))
        .astype(jnp.bfloat16)
    )


def block_sum(field):
    rows, cols, chans = field.shape
    return field.astype(jnp.float32).reshape(rows // 2, 2, cols // 2, 2, chans).sum(axis=(1, 3))


def double_spatial_lattice(field):
    return jnp.repeat(jnp.repeat(field, 2, axis=0), 2, axis=1)


def up_mix(field, matrix):
    taps = jnp.broadcast_to(matrix, (2, 2) + matrix.shape)
    return lax.conv_general_dilated(
        field[None],
        taps,
        window_strides=(1, 1),
        padding=((1, 1), (1, 1)),
        lhs_dilation=(2, 2),
        dimension_numbers=("NHWC", "HWIO", "NHWC"),
        preferred_element_type=jnp.float32,
    )[0]


def pointwise_mixing_weights(field, matrix):
    rows, cols, chans = field.shape
    return jnp.dot(
        field.reshape(rows * cols, chans), matrix, preferred_element_type=jnp.float32
    ).reshape(rows, cols, -1)


def project_back(field, matrix):
    rows, cols, chans = field.shape
    out = lax.dot_general(
        field.reshape(rows * cols, chans),
        matrix,
        (((1,), (1,)), ((), ())),
        preferred_element_type=jnp.float32,
    )
    return out.reshape(rows, cols, -1)


def silu_slope(value):
    sig = jax.nn.sigmoid(value)
    return sig * (1.0 + value * (1.0 - sig))


def inside(padded):
    ok = []
    for axis, dim in (("gy", 0), ("gx", 1)):
        length = padded.shape[dim] - 2
        place = lax.axis_index(axis) * length - 1 + jnp.arange(length + 2)
        ok.append((place >= 0) & (place < length * lax.axis_size(axis)))
    return (ok[0][:, None] & ok[1][None, :])[:, :, None]


def backward_start(cotangent, central_lifted_mixing):
    back_mid = block_sum(cotangent).astype(jnp.bfloat16)
    grad_mid = project_back(back_mid, central_lifted_mixing)
    return grad_mid, block_sum(grad_mid).astype(jnp.bfloat16)


def shards(
    features,
    station_mask,
    station_gain,
    fine_kernel,
    down_mid,
    mid_kernel,
    down_coarse,
    coarse_kernel,
    up_coarse,
    central_lifted_mixing,
    cotangent,
):
    inputs = (
        features.astype(jnp.float32)
        + station_mask.astype(jnp.float32)[:, :, None] * station_gain[None, None, :]
    ).astype(jnp.bfloat16)
    grad_mid, back_coarse = backward_start(cotangent, central_lifted_mixing)
    wide, back_strip = with_halo_and_strip(inputs, 3, back_coarse, 1, 0)
    in_pad = wide[2:-2, 2:-2]
    pre_wide = conv_valid(wide, fine_kernel)
    pre_fine = pre_wide[2:-2, 2:-2]
    act_wide = jax.nn.silu(pre_wide).astype(jnp.bfloat16)
    sharpest_level_response = act_wide[2:-2, 2:-2]
    mid_in = pointwise_mixing_weights(pool_mean(act_wide), down_mid).astype(
        jnp.bfloat16
    )
    pre_mid = conv_valid(jnp.where(inside(mid_in), mid_in, jnp.zeros((), mid_in.dtype)), mid_kernel)
    act_mid = jax.nn.silu(pre_mid).astype(jnp.bfloat16)
    x = lax.axis_index("gx")
    nx = lax.axis_size("gx")
    own_chans = coarse_kernel.shape[3]
    own_up = lax.dynamic_slice_in_dim(up_coarse, x * own_chans, own_chans, axis=0)
    pooled_mid = pool_mean(act_mid)
    rows, cols, _ = pooled_mid.shape
    strip = gather_strip(pooled_mid, 2, 2)
    coarse_in = pointwise_mixing_weights(strip, down_coarse).astype(jnp.bfloat16)
    pre_coarse = conv_valid(coarse_in, coarse_kernel, 1)
    act_own = jax.nn.silu(pre_coarse[1 : 1 + rows]).astype(jnp.bfloat16)
    delta_coarse = (
        project_back(back_strip, own_up) * silu_slope(pre_coarse)
    ).astype(jnp.bfloat16)
    into_own = convt_valid(
        delta_coarse, coarse_kernel, 1
    ).astype(jnp.bfloat16)
    down_own = project_back(into_own, down_coarse).astype(jnp.bfloat16)

    def by_column(field):
        parts = field.reshape(rows, nx, cols, -1).transpose(1, 0, 2, 3)
        return parts.reshape(nx, rows * cols, -1)

    down_parts = swap_blocks(by_column(down_own), 3)
    down_back = down_parts.astype(jnp.float32).sum(axis=0).reshape(rows, cols, -1)
    delta_mid = (
        (grad_mid + double_spatial_lattice(down_back) * 0.25)
        * silu_slope(pre_mid)
    ).astype(jnp.bfloat16)
    into_mid = convt_valid(with_halo(delta_mid, 4), mid_kernel).astype(jnp.bfloat16)
    delta_fine = (
        (
            cotangent.astype(jnp.float32)
            + up_mix(into_mid, down_mid.T) * 0.25
        )
        * silu_slope(pre_fine)
    ).astype(jnp.bfloat16)
    local_grad = kernel_grad(in_pad, delta_fine)
    cells_all = features.shape[0] * lax.axis_size("gy") * features.shape[1] * lax.axis_size("gx")
    scale = 1.0 / jnp.sqrt(jnp.float32(cells_all))
    grad_sum, delta_pad, act_parts = sum_all_with_halo(
        local_grad, delta_fine, by_column(act_own), 6
    )
    act_coarse = act_parts.transpose(1, 0, 2).reshape(rows, cols, nx * own_chans)
    ascend_central_level = (
        up_mix(act_coarse, up_coarse)
        + act_mid.astype(jnp.float32)
    ).astype(jnp.bfloat16)
    predicted_rainfall = (
        up_mix(ascend_central_level, central_lifted_mixing)
        + sharpest_level_response.astype(jnp.float32)
    ).astype(jnp.bfloat16)
    sharpest_filter_derivative = grad_sum.astype(jnp.float32) * scale
    hidden_maps_sensitivity = convt_valid(delta_pad, fine_kernel).astype(jnp.bfloat16)
    return (predicted_rainfall, hidden_maps_sensitivity, sharpest_filter_derivative)


def solution(mesh):
    return jax.shard_map(
        shards,
        mesh=mesh,
        in_specs=(
            P("gy", "gx", None),
            P("gy", "gx"),
            P(),
            P(),
            P(),
            P(),
            P(),
            P(None, None, None, "gx"),
            P(),
            P(),
            P("gy", "gx", None),
        ),
        out_specs=(P("gy", "gx", None), P("gy", "gx", None), P()),
        check_vma=False,
    )
```
